1024 devices in a mesh: section: 32 (over x, z_hi, core), expert: 32 (over y, z_lo).
Axes of the slice: x: 4, y: 4, z: 32 (z_hi: 4, z_lo: 8; z = z_hi * 8 + z_lo), core: 2. Of those that a mesh axis runs over, the one named last changes fastest.
Arguments:
- cotangent: bfloat16 [32, 512, 2048], P('section', 'expert'), may hold values from -6 to 6
- expert_ids: int32 [32, 512, 8], P('section', 'expert'), may hold values from 0 to 31, all different within a row; in each aligned block of 16 rows (0 to 15, 16 to 31, ..., all dimensions but the last counted through in order) at most 8 rows name the same one
- gate_probs: bfloat16 [32, 512, 8], P('section', 'expert'), may hold values from 0.099609375 to 1
- saved: bfloat16 [32, 32, 256, 1536], P('section', 'expert'), may hold values from -5 to 5
- w_gate: bfloat16 [32, 2048, 768], P('expert'), may hold values from -0.125 to 0.125
- w_up: bfloat16 [32, 2048, 768], P('expert'), may hold values from -0.125 to 0.125
- w_down: bfloat16 [32, 768, 2048], P('expert'), may hold values from -0.21875 to 0.21875
Outputs:
- input_grad: bfloat16 [32, 512, 2048], P('section', 'expert')
The draws below stay inside these ranges and needn't reach their ends.
Inputs may be any that keep to these rules, and one draw needn't show every extreme that they name: `expert_ids`: each token names 8 different experts. Within the 16 tokens of one device (aligned blocks along the token dimension) no expert is named by more than 8 tokens, and in every draw some expert is named by exactly 8 of them.
All inputs are finite; a program needn't handle non-finite values.
Results may differ from the reference program's by a relative error of at most 0.015.
Values may be sent and summed in bfloat16 or wider, within the bound.
No kernel may reach another device: no remote copies, remote signals or barrier semaphores. Data moves between devices by JAX's collectives and lax.ppermute only.
A program may use at most 32 MiB of HBM per device.

```python
import math
import jax
import jax.numpy as jnp
import numpy as np
from jax import lax

D = 2048
FF = 768
TOPK = 8
TOK_DEV = 16
EXPERTS = 32
CAP = 8
SECTIONS = 32
TOKENS = 512


def block_levels(own_key, shape, cuts, smallest, high):
    loudness = 1.0
    for position, blocks in cuts:
        draws = jax.random.uniform(jax.random.fold_in(jax.random.fold_in(own_key, 6), position), (blocks,), jnp.float32, smallest / len(cuts), high / len(cuts))
        loudness = loudness * jnp.repeat(jnp.exp(draws), shape[position] // blocks).reshape((-1,) + (1,) * (len(shape) - 1 - position))
    return loudness


def deal_out(stream_key, own, number, rows, number_of, top, bound, skew):
    ranking = jax.random.permutation(stream_key, number_of)
    crowded, usual = load_shares(number_of, rows * top, bound, skew, True), load_shares(number_of, rows * top, bound, skew, False)
    places = jnp.arange(number_of)

    def named(sizes, offset_by):
        used = int((sizes > 0).sum())
        fixed = max(1, used // 4)
        passed = fixed + (places - fixed + offset_by * (used - fixed)) % max(1, number_of - fixed)
        return jnp.zeros((number_of,), jnp.int32).at[ranking[jnp.where(places < fixed, places, passed)]].set(jnp.asarray(sizes, jnp.int32))

    sizes = jnp.where(number % 4 == 0, named(crowded, number // 4), named(usual, number - number // 4 - 1))
    mixed = jax.random.permutation(jax.random.fold_in(own, 3), number_of)
    donor, receiver = mixed[0:number_of // 2 * 2:2], mixed[1:number_of // 2 * 2:2]
    slack = jnp.minimum(sizes[donor] - 1, bound - sizes[receiver]) // 2
    slack = jnp.where((donor == ranking[0]) | (receiver == ranking[0]) | (sizes[receiver] == 0), 0, jnp.maximum(slack, 0))
    passed = jax.random.randint(jax.random.fold_in(own, 4), (number_of // 2,), 0, 1 << 20) % (slack + 1)
    sizes = sizes.at[donor].add(-passed).at[receiver].add(passed)
    labels = jnp.searchsorted(jnp.cumsum(sizes), jnp.arange(rows * top), side="right").astype(jnp.int32)
    table = labels.reshape(top, rows).T
    table = table[jax.random.permutation(jax.random.fold_in(own, 1), rows)]
    offset_by = jax.random.randint(jax.random.fold_in(own, 2), (rows, 1), 0, top)
    return jnp.take_along_axis(table, (jnp.arange(top)[None, :] + offset_by) % top, axis=1)


def load_shares(amount, total, most, skew, full):
    loads = [(1 << 20) // math.isqrt(rank ** skew) + 1 for rank in range(1, amount + 1)]
    largest = most if full else min(most, max(-(-total // amount), total * loads[0] // sum(loads)))
    least = 1 if total - largest >= amount - 1 else 0
    given, spare = [largest] + [least] * (amount - 1), total - largest - least * (amount - 1)
    while spare > 0:
        free = [i for i in range(1, amount) if given[i] < largest] or [i for i in range(1, amount) if given[i] < most]
        whole, budget = sum([loads[i] for i in free]), spare
        for i in free:
            more = min(most - given[i], max(1, budget * loads[i] // whole), spare)
            given[i] = given[i] + more
            spare = spare - more
    return np.array(given)


def bell_draw(rng, shape, scale, most, cuts=(), kind=jnp.bfloat16):
    factor_of = block_levels(rng, shape, cuts, -0.22, 0.18) if cuts else 1.0
    entries = jax.random.normal(rng, shape, jnp.float32) * scale * factor_of
    return jnp.minimum(jnp.maximum(entries, -most), most).astype(kind)


def setup_inputs(seed: int = 0) -> dict:
    splits = jax.random.split(jax.random.key(seed), 8)
    cotangent = bell_draw(splits[0], (SECTIONS, TOKENS, D), 1.0, 6.0, ((0, 32), (1, 32)))
    expert_ids_keys = jax.random.split(jax.random.fold_in(splits[1], 1), SECTIONS * TOKENS // TOK_DEV)
    expert_ids_turns = jax.random.permutation(jax.random.fold_in(splits[1], 3), SECTIONS * TOKENS // TOK_DEV)
    expert_ids = jax.vmap(lambda own, number: deal_out(jax.random.fold_in(splits[1], 2), own, number, TOK_DEV, EXPERTS, TOPK, CAP, 2))(expert_ids_keys, expert_ids_turns).reshape((SECTIONS, TOKENS, TOPK))
    gate_probs = jnp.clip(jnp.exp(math.log(1.0) - 2.306499 * jax.random.uniform(splits[2], (SECTIONS, TOKENS, TOPK), jnp.float32) ** block_levels(splits[2], (SECTIONS, TOKENS, TOPK), ((0, 32), (1, 32)), -0.2, 0.2)), 0.099609375, 1.0).astype(jnp.bfloat16)
    saved = bell_draw(splits[3], (SECTIONS, EXPERTS, EXPERTS * CAP, 2 * FF), 1.0, 5.0, ((0, 32), (1, 32)))
    w_gate = bell_draw(splits[4], (EXPERTS, D, FF), D ** -0.5, 0.125, ((0, 32),))
    w_up = bell_draw(splits[5], (EXPERTS, D, FF), D ** -0.5, 0.125, ((0, 32),))
    w_down = bell_draw(splits[6], (EXPERTS, FF, D), FF ** -0.5, 0.21875, ((0, 32),))
    return dict(cotangent=cotangent, expert_ids=expert_ids, gate_probs=gate_probs, saved=saved, w_gate=w_gate, w_up=w_up, w_down=w_down)


def slot_grad(slot_rows, slot_share, kept_acts, gate_mat, up_mat, down_mat):
    hidden_grad = jnp.dot(slot_rows, down_mat.T, preferred_element_type=jnp.float32)
    hidden_grad = hidden_grad * slot_share.astype(jnp.float32)[:, None]
    width = gate_mat.shape[1]
    pre_gate = kept_acts[:, :width].astype(jnp.float32)
    pre_up = kept_acts[:, width:].astype(jnp.float32)
    gate_sig = jax.nn.sigmoid(pre_gate)
    up_grad = (hidden_grad * pre_gate * gate_sig).astype(jnp.bfloat16)
    gate_grad = (hidden_grad * pre_up * gate_sig * (1.0 + pre_gate * (1.0 - gate_sig))).astype(jnp.bfloat16)
    summed = jnp.dot(gate_grad, gate_mat.T, preferred_element_type=jnp.float32)
    summed = summed + jnp.dot(up_grad, up_mat.T, preferred_element_type=jnp.float32)
    return summed.astype(jnp.bfloat16)

def reference(cotangent, expert_ids, gate_probs, saved, w_gate, w_up, w_down):
    incoming_all = jnp.roll(cotangent, -1, axis=0)

    def one_section(section_args):
        incoming, route_ids, route_probs, kept_section = section_args
        incoming = incoming.reshape(EXPERTS, TOK_DEV, D)
        route_ids = route_ids.reshape(EXPERTS, TOK_DEV, TOPK)
        route_probs = route_probs.reshape(EXPERTS, TOK_DEV, TOPK)
        matches = route_ids[..., None] == jnp.arange(EXPERTS, dtype=jnp.int32)[None, None, None, :]
        member = jnp.any(matches, axis=2).astype(jnp.int32)
        shares = lax.optimization_barrier(jnp.sum(jnp.where(matches, route_probs.astype(jnp.float32)[..., None], jnp.float32(0.0)), axis=2))
        earlier = jnp.cumsum(member, axis=1, dtype=jnp.int32) - member
        slot_map = (member[..., None] * (earlier[..., None] == jnp.arange(CAP, dtype=jnp.int32)[None, None, None, :])).astype(jnp.float32)
        slot_rows = jnp.einsum('stec,std->escd', slot_map, incoming.astype(jnp.float32)).astype(jnp.bfloat16)
        slot_share = jnp.einsum('stec,ste->esc', slot_map, shares).astype(jnp.bfloat16)

        def one_expert(expert_args):
            rows_e, share_e, kept_e, gate_mat, up_mat, down_mat = expert_args
            grads = slot_grad(rows_e.reshape(EXPERTS * CAP, D), share_e.reshape(EXPERTS * CAP), kept_e, gate_mat, up_mat, down_mat)
            return grads.reshape(EXPERTS, CAP, D)
        returned = lax.map(one_expert, (slot_rows, slot_share, kept_section, w_gate, w_up, w_down))
        total = jnp.einsum('stec,escd->std', slot_map, returned.astype(jnp.float32))
        return total.astype(jnp.bfloat16).reshape(TOKENS, D)
    return lax.map(one_section, (incoming_all, expert_ids, gate_probs, saved))
```

```python
import jax
import jax.numpy as jnp
from jax import lax
from jax.experimental import pallas as pl
from jax.experimental.pallas import tpu as pltpu
from jax.sharding import Mesh, PartitionSpec as P

BF = jnp.bfloat16
F32 = jnp.float32
YS = 4
ZS = 8


def call(kernel, outs, limit, cost):
    return pl.pallas_call(
        kernel,
        out_shape=outs,
        compiler_params=pltpu.CompilerParams(vmem_limit_bytes=limit),
        cost_estimate=pl.CostEstimate(flops=cost[0], bytes_accessed=cost[1], transcendentals=0),
    )


def iota(shape, dim):
    return lax.broadcasted_iota(jnp.int32, shape, dim)


def shares_kernel(ids_ref, probs_ref, out_ref):
    rows, tokens = out_ref.shape
    r = iota((rows, tokens), 0)
    expert = (r % YS) * ZS + r // YS
    acc = jnp.zeros((rows, tokens), F32)
    for k in range(ids_ref.shape[0]):
        acc = acc + jnp.where(ids_ref[k : k + 1, :] == expert, probs_ref[k : k + 1, :].astype(F32), 0.0)
    out_ref[...] = acc.astype(BF)


def dot(a, b, dims=((1,), (0,))):
    return lax.dot_general(a, b, (dims, ((), ())), preferred_element_type=F32)


def maps_kernel(cap, share_ref, pick_ref, give_ref):
    slots, toks = pick_ref.shape
    rows, own = share_ref.shape
    share = share_ref[...]
    r = iota((slots, rows), 0)
    k = iota((slots, rows), 1)
    place = ((r // cap) % ZS) * YS + r // (cap * ZS)
    spread_rows = jnp.where(place == k, 1.0, 0.0).astype(BF)
    per_slot = dot(spread_rows, share)
    member = jnp.where(per_slot > 0, 1.0, 0.0).astype(BF)
    before = jnp.where(iota((own, own), 0) < iota((own, own), 1), 1.0, 0.0).astype(BF)
    earlier = dot(member, before)
    spread = jnp.where(iota((own, toks), 0) == iota((own, toks), 1) % own, 1.0, 0.0).astype(BF)
    share_at = dot(per_slot.astype(BF), spread)
    earlier_at = dot(earlier.astype(BF), spread)
    rr = iota((slots, toks), 0)
    tt = iota((slots, toks), 1)
    hit = (share_at > 0) & (tt // own == (rr // cap) % ZS) & (earlier_at == (rr % cap).astype(F32))
    pick_ref[...] = jnp.where(hit, 1.0, 0.0).astype(BF)
    give_ref[...] = jnp.where(hit, share_at, 0.0).astype(BF)


def compress_kernel(pick_ref, rows_ref, out_ref):
    out_ref[...] = dot(pick_ref[...], rows_ref[...]).astype(BF)


def combine_kernel(give_ref, rows_ref, out_ref):
    out_ref[...] = dot(give_ref[...], rows_ref[...], ((0,), (0,))).astype(BF)


def expert_kernel(rows_ref, kept_ref, gate_ref, up_ref, down_ref, out_ref):
    width = gate_ref.shape[1]
    hidden = dot(rows_ref[...], down_ref[...], ((1,), (1,)))
    g = kept_ref[:, :width].astype(F32)
    u = kept_ref[:, width:].astype(F32)
    s = jax.nn.sigmoid(g)
    hs = hidden * s
    up_grad = (hs * g).astype(BF)
    gate_grad = (hs * u * (1.0 + g * (1.0 - s))).astype(BF)
    total = dot(gate_grad, gate_ref[...], ((1,), (1,))) + dot(up_grad, up_ref[...], ((1,), (1,)))
    out_ref[...] = total.astype(BF)


def total_kernel(parts_ref, out_ref):
    acc = parts_ref[0].astype(F32)
    for k in range(1, parts_ref.shape[0]):
        acc = acc + parts_ref[k].astype(F32)
    out_ref[...] = acc.astype(BF)


def body(cotangent, expert_ids, gate_probs, saved, w_gate, w_up, w_down):
    sections = lax.axis_size("section")
    tokens, width = cotangent.shape[1:]
    slots = saved.shape[2]
    cap = slots // (YS * ZS)
    mib = 1 << 20
    incoming = lax.ppermute(cotangent[0], "section", [(i, (i - 1) % sections) for i in range(sections)])
    shares = call(shares_kernel, jax.ShapeDtypeStruct((YS * ZS, tokens), BF), 4 * mib, (10**5, 10**4))(
        expert_ids[0].T, gate_probs[0].T
    )
    shares = lax.all_to_all(shares.reshape(ZS, YS, tokens), "z", 0, 0, tiled=True)
    map_shape = jax.ShapeDtypeStruct((slots, ZS * tokens), BF)
    pick, give = call(
        lambda *refs: maps_kernel(cap, *refs), (map_shape, map_shape), 8 * mib, (10**7, 10**5)
    )(shares.reshape(ZS * YS, tokens))
    spread = jnp.broadcast_to(incoming[None], (ZS, tokens, width))
    row_tokens = lax.all_to_all(spread, "z", 0, 0, tiled=True).reshape(ZS * tokens, width)
    sent = call(compress_kernel, jax.ShapeDtypeStruct((slots, width), BF), 8 * mib, (10**8, 10**6))(pick, row_tokens)
    slot_rows = lax.all_to_all(sent.reshape(YS, -1, width), "y", 0, 0, tiled=True).reshape(slots, width)
    grads = call(expert_kernel, jax.ShapeDtypeStruct((slots, width), BF), 16 * mib, (24 * 10**8, 11 * 10**6))(
        slot_rows, saved[0, 0], w_gate[0], w_up[0], w_down[0]
    )
    back = lax.all_to_all(grads.reshape(YS, -1, width), "y", 0, 0, tiled=True).reshape(slots, width)
    partial = call(combine_kernel, jax.ShapeDtypeStruct((ZS * tokens, width), BF), 8 * mib, (10**8, 10**6))(give, back)
    parts = lax.all_to_all(partial.reshape(ZS, tokens, width), "z", 0, 0, tiled=True)
    out = call(total_kernel, jax.ShapeDtypeStruct((tokens, width), BF), 4 * mib, (10**6, 10**6))(parts)
    return out[None]


def solution(mesh):
    split = Mesh(mesh.devices.reshape(-1, YS, ZS), ("section", "y", "z"))
    over = P("section", ("y", "z"), None)
    weight = P(("y", "z"), None, None)
    in_specs = (over, over, over, P("section", ("y", "z"), None, None), weight, weight, weight)
    return jax.shard_map(body, mesh=split, in_specs=in_specs, out_specs=over, check_vma=False)
```

```python
import jax
import jax.numpy as jnp
from jax import lax
from jax.experimental import pallas as pl
from jax.experimental.pallas import tpu as pltpu
from jax.sharding import Mesh, PartitionSpec as P

BF = jnp.bfloat16
F32 = jnp.float32
YS = 4
ZS = 8
QUAD = 4


def call(kernel, outs, limit, cost):
    return pl.pallas_call(
        kernel,
        out_shape=outs,
        compiler_params=pltpu.CompilerParams(vmem_limit_bytes=limit),
        cost_estimate=pl.CostEstimate(flops=cost[0], bytes_accessed=cost[1], transcendentals=0),
    )


def iota(shape, dim):
    return lax.broadcasted_iota(jnp.int32, shape, dim)


def shares_kernel(ids_ref, probs_ref, out_ref):
    rows, tokens = out_ref.shape
    r = iota((rows, tokens), 0)
    expert = (r % YS) * ZS + r // YS
    acc = jnp.zeros((rows, tokens), F32)
    for k in range(ids_ref.shape[0]):
        acc = acc + jnp.where(ids_ref[k : k + 1, :] == expert, probs_ref[k : k + 1, :].astype(F32), 0.0)
    out_ref[...] = acc.astype(BF)


def dot(a, b, dims=((1,), (0,))):
    return lax.dot_general(a, b, (dims, ((), ())), preferred_element_type=F32)


def maps_kernel(cap, share_ref, pick_ref, give_ref):
    slots, toks = pick_ref.shape
    rows, own = share_ref.shape
    share = share_ref[...]
    r = iota((slots, rows), 0)
    k = iota((slots, rows), 1)
    place = ((r // cap) % ZS) * YS + r // (cap * ZS)
    spread_rows = jnp.where(place == k, 1.0, 0.0).astype(BF)
    per_slot = dot(spread_rows, share)
    member = jnp.where(per_slot > 0, 1.0, 0.0).astype(BF)
    before = jnp.where(iota((own, own), 0) < iota((own, own), 1), 1.0, 0.0).astype(BF)
    earlier = dot(member, before)
    spread = jnp.where(iota((own, toks), 0) == iota((own, toks), 1) % own, 1.0, 0.0).astype(BF)
    share_at = dot(per_slot.astype(BF), spread)
    earlier_at = dot(earlier.astype(BF), spread)
    rr = iota((slots, toks), 0)
    block = iota((slots, toks), 1) // own
    mine = lax.axis_index("zh") * QUAD
    block_z = jnp.where(block < QUAD, mine + block, (ZS - QUAD - mine) + (block - QUAD))
    hit = (share_at > 0) & (block_z == (rr // cap) % ZS) & (earlier_at == (rr % cap).astype(F32))
    pick_ref[...] = jnp.where(hit, 1.0, 0.0).astype(BF)
    give_ref[...] = jnp.where(hit, share_at, 0.0).astype(BF)


def compress_kernel(pick_ref, mine_ref, other_ref, out_ref):
    half = mine_ref.shape[0]
    out_ref[...] = (dot(pick_ref[:, :half], mine_ref[...]) + dot(pick_ref[:, half:], other_ref[...])).astype(BF)


def combine_kernel(give_ref, rows_ref, mine_ref, other_ref):
    half = mine_ref.shape[0]
    rows = rows_ref[...]
    other_ref[...] = dot(give_ref[:, half:], rows, ((0,), (0,))).astype(BF)
    mine_ref[...] = dot(give_ref[:, :half], rows, ((0,), (0,))).astype(BF)


def expert_kernel(rows_ref, kept_hbm, gate_hbm, up_hbm, down_hbm, out_ref, kept, gate, up, down, hidden, sems):
    ff, width = down.shape
    copies = []

    def fetch(src, dst, parts):
        step = src.shape[0] // parts
        begun = []
        for k in range(parts):
            rows = pl.ds(k * step, step)
            copy = pltpu.make_async_copy(src.at[rows], dst.at[rows], sems.at[len(copies)])
            copy.start()
            copies.append(copy)
            begun.append((copy, rows))
        return begun

    down_parts = fetch(down_hbm, down, 3)
    kept_parts = fetch(kept_hbm, kept, 1)
    pairs = []
    step = width // 4
    for k in range(4):
        rows = pl.ds(k * step, step)
        for src, dst in ((gate_hbm, gate), (up_hbm, up)):
            copy = pltpu.make_async_copy(src.at[rows], dst.at[rows], sems.at[len(copies)])
            copy.start()
            copies.append(copy)
            pairs.append(copy)
    rows = rows_ref[...]
    for copy, part in down_parts:
        copy.wait()
        hidden[:, part] = dot(rows, down[part, :], ((1,), (1,)))
    for copy, _ in kept_parts:
        copy.wait()
    h = hidden[...]
    g = kept[:, :ff].astype(F32)
    u = kept[:, ff:].astype(F32)
    s = jax.nn.sigmoid(g)
    hs = h * s
    up_grad = (hs * g).astype(BF)
    gate_grad = (hs * u * (1.0 + g * (1.0 - s))).astype(BF)
    for k in range(4):
        pairs[2 * k].wait()
        pairs[2 * k + 1].wait()
        part = pl.ds(k * step, step)
        total = dot(gate_grad, gate[part, :], ((1,), (1,))) + dot(up_grad, up[part, :], ((1,), (1,)))
        out_ref[:, part] = total.astype(BF)


def sum_of(parts_ref):
    acc = parts_ref[0].astype(F32)
    for k in range(1, parts_ref.shape[0]):
        acc = acc + parts_ref[k].astype(F32)
    return acc


def half_kernel(parts_ref, out_ref):
    out_ref[...] = sum_of(parts_ref).astype(BF)


def total_kernel(parts_ref, far_ref, out_ref):
    out_ref[...] = (sum_of(parts_ref) + far_ref[...].astype(F32)).astype(BF)


def swapped(x):
    return lax.ppermute(x, "zh", [(0, 1), (1, 0)])


def quad(x):
    return lax.all_to_all(x, "zl", 0, 0, tiled=True)


def body(cotangent, expert_ids, gate_probs, saved, w_gate, w_up, w_down):
    sections = lax.axis_size("section")
    tokens, width = cotangent.shape[1:]
    slots = saved.shape[2]
    cap = slots // (YS * ZS)
    half = QUAD * tokens
    mib = 1 << 20
    incoming = lax.ppermute(cotangent[0], "section", [(i, (i - 1) % sections) for i in range(sections)])
    shares = call(shares_kernel, jax.ShapeDtypeStruct((YS * ZS, tokens), BF), 4 * mib, (10**5, 10**4))(
        expert_ids[0].T, gate_probs[0].T
    )
    shares = lax.all_to_all(shares.reshape(ZS, YS, tokens), ("zh", "zl"), 0, 0, tiled=True)
    map_shape = jax.ShapeDtypeStruct((slots, ZS * tokens), BF)
    pick, give = call(
        lambda *refs: maps_kernel(cap, *refs), (map_shape, map_shape), 8 * mib, (10**7, 10**5)
    )(shares.reshape(ZS * YS, tokens))
    crossed = swapped(incoming)
    mine = quad(jnp.broadcast_to(incoming[None], (QUAD, tokens, width)))
    other = quad(jnp.broadcast_to(crossed[None], (QUAD, tokens, width)))
    sent = call(compress_kernel, jax.ShapeDtypeStruct((slots, width), BF), 8 * mib, (10**8, 10**6))(
        pick, mine.reshape(half, width), other.reshape(half, width)
    )
    slot_rows = lax.all_to_all(sent.reshape(YS, -1, width), "y", 0, 0, tiled=True).reshape(slots, width)
    arrays = (saved[0, 0], w_gate[0], w_up[0], w_down[0])
    vm = pl.BlockSpec(memory_space=pltpu.VMEM)
    grads = pl.pallas_call(
        expert_kernel,
        out_shape=jax.ShapeDtypeStruct((slots, width), BF),
        in_specs=[vm] + [pl.BlockSpec(memory_space=pltpu.HBM)] * 4,
        out_specs=vm,
        scratch_shapes=[pltpu.VMEM(x.shape, x.dtype) for x in arrays]
        + [pltpu.VMEM((slots, w_down.shape[1]), F32), pltpu.SemaphoreType.DMA((12,))],
        compiler_params=pltpu.CompilerParams(vmem_limit_bytes=48 * mib),
        cost_estimate=pl.CostEstimate(flops=24 * 10**8, bytes_accessed=12 * 10**6, transcendentals=0),
    )(slot_rows, *arrays)
    back = lax.all_to_all(grads.reshape(YS, -1, width), "y", 0, 0, tiled=True).reshape(slots, width)
    half_shape = jax.ShapeDtypeStruct((half, width), BF)
    own_part, far_part = call(combine_kernel, (half_shape, half_shape), 8 * mib, (10**8, 10**6))(give, back)
    far = quad(far_part.reshape(QUAD, tokens, width))
    far = swapped(call(half_kernel, jax.ShapeDtypeStruct((tokens, width), BF), 4 * mib, (10**6, 10**6))(far))
    own = quad(own_part.reshape(QUAD, tokens, width))
    out = call(total_kernel, jax.ShapeDtypeStruct((tokens, width), BF), 4 * mib, (10**6, 10**6))(own, far)
    return out[None]


def solution(mesh):
    split = Mesh(mesh.devices.reshape(-1, YS, ZS // QUAD, QUAD), ("section", "y", "zh", "zl"))
    line = ("y", "zh", "zl")
    over = P("section", line, None)
    weight = P(line, None, None)
    in_specs = (over, over, over, P("section", line, None, None), weight, weight, weight)
    return jax.shard_map(body, mesh=split, in_specs=in_specs, out_specs=over, check_vma=False)
```

```python
import jax
import jax.numpy as jnp
from jax import lax
from jax.experimental import pallas as pl
from jax.experimental.pallas import tpu as pltpu
from jax.sharding import Mesh, PartitionSpec as P

BF = jnp.bfloat16
F32 = jnp.float32
YS = 4
ZS = 8
QUAD = 4
LANES = 128
MIB = 1 << 20
PARTS = 2


def call(kernel, outs, limit, cost):
    return pl.pallas_call(
        kernel,
        out_shape=outs,
        compiler_params=pltpu.CompilerParams(vmem_limit_bytes=limit * MIB),
        cost_estimate=pl.CostEstimate(flops=cost[0], bytes_accessed=cost[1], transcendentals=0),
    )


def bf16(*shape):
    return jax.ShapeDtypeStruct(shape, BF)


def iota(shape, dim):
    return lax.broadcasted_iota(jnp.int32, shape, dim)


def dot(a, b, dims=((1,), (0,))):
    return lax.dot_general(a, b, (dims, ((), ())), preferred_element_type=F32)


def flag(mask):
    return jnp.where(mask, 1.0, 0.0).astype(BF)


def shares_kernel(ids_ref, probs_ref, out_ref):
    shape = out_ref.shape
    expert = iota(shape, 1)
    acc = jnp.zeros(shape, F32)
    for k in range(ids_ref.shape[1]):
        acc = acc + jnp.where(ids_ref[:, k : k + 1] == expert, probs_ref[:, k : k + 1].astype(F32), 0.0)
    out_ref[...] = acc.astype(BF)


def payload_kernel(rows_ref, share_ref, quad_ref, one_ref):
    width = rows_ref.shape[1]
    one_ref[:, :width] = rows_ref[...]
    one_ref[:, width:] = share_ref[...]
    for k in range(QUAD):
        quad_ref[k, :, :width] = rows_ref[...]
        quad_ref[k, :, width:] = share_ref[...]


def pack_kernel(cap, own, near_ref, far_ref, sent_ref, give_ref):
    _, slots, toks = give_ref.shape
    width = sent_ref.shape[3]
    mine = lax.axis_index("zh")
    z = mine * QUAD + lax.axis_index("zl")
    r = iota((slots, LANES), 0)
    wanted = flag((r // (cap * QUAD)) * ZS + z == iota((slots, LANES), 1))
    i, j = iota((toks, toks), 0), iota((toks, toks), 1)
    before = flag((i < j) & (i // own == j // own))
    rr, tt = iota((slots, toks), 0), iota((slots, toks), 1)
    for k, rows_ref in enumerate((near_ref, far_ref)):
        share_at = dot(wanted, rows_ref[:, width:], ((1,), (1,)))
        earlier = dot(flag(share_at > 0), before)
        hit = (share_at > 0) & (tt // own == (rr // cap) % QUAD) & (earlier == (rr % cap).astype(F32))
        give_ref[k] = jnp.where(hit, share_at, 0.0).astype(BF)
        packed = dot(flag(hit), rows_ref[:, :width]).astype(BF)
        sent_ref[:, pl.ds((mine + k) % 2, 1)] = packed.reshape(YS, 1, slots // YS, width)


def combine_kernel(give_ref, rows_ref, near_ref, far_ref):
    mine = lax.axis_index("zh")
    slots = give_ref.shape[1]
    for k, out_ref in ((1, far_ref), (0, near_ref)):
        rows = rows_ref[:, pl.ds((mine + k) % 2, 1)].reshape(slots, -1)
        out_ref[...] = dot(give_ref[k], rows, ((0,), (0,))).astype(BF)


def expert_kernel(rows_ref, kept_ref, gate_ref, up_hbm, down_hbm, out_ref, up, down, hidden, sems):
    ff, width = down.shape
    parts = sems.shape[0] // 2
    begun = []
    for src, dst in ((down_hbm, down), (up_hbm, up)):
        step = src.shape[0] // parts
        for k in range(parts):
            at = pl.ds(k * step, step)
            copy = pltpu.make_async_copy(src.at[at], dst.at[at], sems.at[len(begun)])
            copy.start()
            begun.append((copy, at))
    for copy, at in begun[:parts]:
        copy.wait()
        hidden[:, at] = dot(rows_ref[...], down[at, :], ((1,), (1,)))
    h = hidden[...]
    g = kept_ref[:, :ff].astype(F32)
    u = kept_ref[:, ff:].astype(F32)
    s = jax.nn.sigmoid(g)
    hs = h * s
    up_grad = (hs * g).astype(BF)
    gate_grad = (hs * u * (1.0 + g * (1.0 - s))).astype(BF)
    for copy, at in begun[parts:]:
        copy.wait()
        total = dot(gate_grad, gate_ref[at, :], ((1,), (1,))) + dot(up_grad, up[at, :], ((1,), (1,)))
        out_ref[:, at] = total.astype(BF)


def sum_of(parts_ref):
    acc = parts_ref[0].astype(F32)
    for k in range(1, parts_ref.shape[0]):
        acc = acc + parts_ref[k].astype(F32)
    return acc


def half_kernel(parts_ref, out_ref):
    out_ref[...] = sum_of(parts_ref).astype(BF)


def total_kernel(parts_ref, far_ref, out_ref):
    out_ref[...] = (sum_of(parts_ref) + far_ref[...].astype(F32)).astype(BF)


def swapped(x):
    return lax.ppermute(x, "zh", [(0, 1), (1, 0)])


def quad(x):
    return lax.all_to_all(x, "zl", 0, 0, tiled=True)


def across(x):
    return lax.all_to_all(x.reshape(YS, -1, x.shape[-1]), "y", 0, 0, tiled=True).reshape(x.shape)


def body(cotangent, expert_ids, gate_probs, saved, w_gate, w_up, w_down):
    sections = lax.axis_size("section")
    tokens, width = cotangent.shape[1:]
    slots = saved.shape[2]
    cap = slots // (YS * ZS)
    half = QUAD * tokens
    incoming = lax.ppermute(cotangent[0], "section", [(i, (i - 1) % sections) for i in range(sections)])
    shares = call(shares_kernel, bf16(tokens, LANES), 4, (10**5, 10**4))(expert_ids[0], gate_probs[0])
    copies, one = call(
        payload_kernel, (bf16(QUAD, tokens, width + LANES), bf16(tokens, width + LANES)), 4, (10**5, 10**6)
    )(incoming, shares)
    crossed = swapped(one)
    near_rows = quad(copies)
    far_rows = quad(jnp.broadcast_to(crossed[None], (QUAD, tokens, width + LANES)))
    sent, give = call(
        lambda *refs: pack_kernel(cap, tokens, *refs),
        (bf16(YS, 2, slots // (2 * YS), width), bf16(2, slots // 2, half)),
        8,
        (10**8, 10**6),
    )(near_rows.reshape(half, -1), far_rows.reshape(half, -1))
    vm = pl.BlockSpec(memory_space=pltpu.VMEM)
    anywhere = pl.BlockSpec(memory_space=pl.ANY)
    grads = pl.pallas_call(
        expert_kernel,
        out_shape=bf16(slots, width),
        in_specs=[vm, vm, vm, anywhere, anywhere],
        out_specs=vm,
        scratch_shapes=[
            pltpu.VMEM(w_up.shape[1:], BF),
            pltpu.VMEM(w_down.shape[1:], BF),
            pltpu.VMEM((slots, w_down.shape[1]), F32),
            pltpu.SemaphoreType.DMA((2 * PARTS,)),
        ],
        compiler_params=pltpu.CompilerParams(vmem_limit_bytes=48 * MIB),
        cost_estimate=pl.CostEstimate(flops=24 * 10**8, bytes_accessed=12 * 10**6, transcendentals=0),
    )(across(sent).reshape(slots, width), saved[0, 0], w_gate[0], w_up[0], w_down[0])
    back = across(grads).reshape(sent.shape)
    near, far = call(combine_kernel, (bf16(half, width), bf16(half, width)), 8, (10**8, 10**6))(give, back)
    far = quad(far.reshape(QUAD, tokens, width))
    far = swapped(call(half_kernel, bf16(tokens, width), 4, (10**6, 10**6))(far))
    near = quad(near.reshape(QUAD, tokens, width))
    out = call(total_kernel, bf16(tokens, width), 4, (10**6, 10**6))(near, far)
    return out[None]


def solution(mesh):
    split = Mesh(mesh.devices.reshape(-1, YS, ZS // QUAD, QUAD), ("section", "y", "zh", "zl"))
    line = ("y", "zh", "zl")
    over = P("section", line, None)
    weight = P(line, None, None)
    in_specs = (over, over, over, P("section", line, None, None), weight, weight, weight)
    return jax.shard_map(body, mesh=split, in_specs=in_specs, out_specs=over, check_vma=False)
```

```python
import jax
import jax.numpy as jnp
from jax import lax
from jax.experimental import pallas as pl
from jax.experimental.pallas import tpu as pltpu
from jax.sharding import Mesh, PartitionSpec as P

BF = jnp.bfloat16
F32 = jnp.float32
YS = 4
ZS = 8
QUAD = 4
LANES = 128
MIB = 1 << 20
PARTS = 2


def call(kernel, outs, limit, cost):
    return pl.pallas_call(
        kernel,
        out_shape=outs,
        compiler_params=pltpu.CompilerParams(vmem_limit_bytes=limit * MIB),
        cost_estimate=pl.CostEstimate(flops=cost[0], bytes_accessed=cost[1], transcendentals=0),
    )


def bf16(*shape):
    return jax.ShapeDtypeStruct(shape, BF)


def iota(shape, dim):
    return lax.broadcasted_iota(jnp.int32, shape, dim)


def dot(a, b, dims=((1,), (0,))):
    return lax.dot_general(a, b, (dims, ((), ())), preferred_element_type=F32)


def flag(mask):
    return jnp.where(mask, 1.0, 0.0).astype(BF)


def shares_kernel(ids_ref, probs_ref, out_ref):
    shape = out_ref.shape
    expert = iota(shape, 1)
    acc = jnp.zeros(shape, F32)
    for k in range(ids_ref.shape[1]):
        acc = acc + jnp.where(ids_ref[:, k : k + 1] == expert, probs_ref[:, k : k + 1].astype(F32), 0.0)
    out_ref[...] = acc.astype(BF)


def payload_kernel(near_ref, far_ref, near_share_ref, far_share_ref, out_ref):
    own, width = near_ref.shape
    for k in range(QUAD):
        out_ref[k, :own, :width] = near_ref[...]
        out_ref[k, own:, :width] = far_ref[...]
        out_ref[k, :own, width:] = near_share_ref[...]
        out_ref[k, own:, width:] = far_share_ref[...]


def pack_kernel(cap, own, rows_ref, sent_ref, give_ref):
    _, slots, toks = give_ref.shape
    width = sent_ref.shape[3]
    mine = lax.axis_index("zh")
    z = mine * QUAD + lax.axis_index("zl")
    r = iota((slots, LANES), 0)
    wanted = flag((r // (cap * QUAD)) * ZS + z == iota((slots, LANES), 1))
    i, j = iota((toks, toks), 0), iota((toks, toks), 1)
    before = flag((i < j) & (i // own == j // own))
    rr, tt = iota((slots, toks), 0), iota((slots, toks), 1)
    for k in range(2):
        rows = rows_ref[:, k * own : (k + 1) * own, :].reshape(toks, -1)
        share_at = dot(wanted, rows[:, width:], ((1,), (1,)))
        earlier = dot(flag(share_at > 0), before)
        hit = (share_at > 0) & (tt // own == (rr // cap) % QUAD) & (earlier == (rr % cap).astype(F32))
        give_ref[k] = jnp.where(hit, share_at, 0.0).astype(BF)
        packed = dot(flag(hit), rows[:, :width]).astype(BF)
        sent_ref[:, pl.ds((mine + k) % 2, 1)] = packed.reshape(YS, 1, slots // YS, width)


def combine_kernel(give_ref, rows_ref, out_ref):
    mine = lax.axis_index("zh")
    slots = give_ref.shape[1]
    own = out_ref.shape[1] // 2
    for k in range(2):
        rows = rows_ref[:, pl.ds((mine + k) % 2, 1)].reshape(slots, -1)
        part = dot(give_ref[k], rows, ((0,), (0,))).astype(BF)
        out_ref[:, k * own : (k + 1) * own] = part.reshape(QUAD, own, -1)


def expert_kernel(rows_ref, kept_ref, gate_ref, up_hbm, down_hbm, out_ref, up, down, hidden, sems):
    ff, width = down.shape
    parts = sems.shape[0] // 2
    begun = []
    for src, dst in ((down_hbm, down), (up_hbm, up)):
        step = src.shape[0] // parts
        for k in range(parts):
            at = pl.ds(k * step, step)
            copy = pltpu.make_async_copy(src.at[at], dst.at[at], sems.at[len(begun)])
            copy.start()
            begun.append((copy, at))
    for copy, at in begun[:parts]:
        copy.wait()
        hidden[:, at] = dot(rows_ref[...], down[at, :], ((1,), (1,)))
    h = hidden[...]
    g = kept_ref[:, :ff].astype(F32)
    u = kept_ref[:, ff:].astype(F32)
    s = jax.nn.sigmoid(g)
    hs = h * s
    up_grad = (hs * g).astype(BF)
    gate_grad = (hs * u * (1.0 + g * (1.0 - s))).astype(BF)
    for copy, at in begun[parts:]:
        copy.wait()
        total = dot(gate_grad, gate_ref[at, :], ((1,), (1,))) + dot(up_grad, up[at, :], ((1,), (1,)))
        out_ref[:, at] = total.astype(BF)


def sum_of(parts_ref, at):
    acc = parts_ref[0, at].astype(F32)
    for k in range(1, parts_ref.shape[0]):
        acc = acc + parts_ref[k, at].astype(F32)
    return acc


def half_kernel(parts_ref, out_ref):
    own = out_ref.shape[0]
    out_ref[...] = sum_of(parts_ref, slice(own, 2 * own)).astype(BF)


def total_kernel(parts_ref, far_ref, out_ref):
    own = out_ref.shape[0]
    out_ref[...] = (sum_of(parts_ref, slice(0, own)) + far_ref[...].astype(F32)).astype(BF)


def swapped(x):
    return lax.ppermute(x, "zh", [(0, 1), (1, 0)])


def quad(x):
    return lax.all_to_all(x, "zl", 0, 0, tiled=True)


def across(x):
    return lax.all_to_all(x.reshape(YS, -1, x.shape[-1]), "y", 0, 0, tiled=True).reshape(x.shape)


def body(cotangent, expert_ids, gate_probs, saved, w_gate, w_up, w_down):
    sections = lax.axis_size("section")
    tokens, width = cotangent.shape[1:]
    slots = saved.shape[2]
    cap = slots // (YS * ZS)
    half = QUAD * tokens
    halves = ZS // QUAD
    moves = [
        ((q * halves + h) * QUAD + k, ((q - 1) % sections * halves + (h + 1) % halves) * QUAD + k)
        for q in range(sections)
        for h in range(halves)
        for k in range(QUAD)
    ]
    crossed = lax.ppermute(cotangent[0], ("section", "zh", "zl"), moves)
    incoming = lax.ppermute(cotangent[0], "section", [(i, (i - 1) % sections) for i in range(sections)])
    shares = call(shares_kernel, bf16(tokens, LANES), 4, (10**5, 10**4))(expert_ids[0], gate_probs[0])
    payload = call(payload_kernel, bf16(QUAD, 2 * tokens, width + LANES), 4, (10**5, 10**6))(
        incoming, crossed, shares, swapped(shares)
    )
    sent, give = call(
        lambda *refs: pack_kernel(cap, tokens, *refs),
        (bf16(YS, 2, slots // (2 * YS), width), bf16(2, slots // 2, half)),
        8,
        (10**8, 10**6),
    )(quad(payload))
    vm = pl.BlockSpec(memory_space=pltpu.VMEM)
    anywhere = pl.BlockSpec(memory_space=pl.ANY)
    grads = pl.pallas_call(
        expert_kernel,
        out_shape=bf16(slots, width),
        in_specs=[vm, vm, vm, anywhere, anywhere],
        out_specs=vm,
        scratch_shapes=[
            pltpu.VMEM(w_up.shape[1:], BF),
            pltpu.VMEM(w_down.shape[1:], BF),
            pltpu.VMEM((slots, w_down.shape[1]), F32),
            pltpu.SemaphoreType.DMA((2 * PARTS,)),
        ],
        compiler_params=pltpu.CompilerParams(vmem_limit_bytes=48 * MIB),
        cost_estimate=pl.CostEstimate(flops=24 * 10**8, bytes_accessed=12 * 10**6, transcendentals=0),
    )(across(sent).reshape(slots, width), saved[0, 0], w_gate[0], w_up[0], w_down[0])
    back = across(grads).reshape(sent.shape)
    parts = quad(call(combine_kernel, bf16(QUAD, 2 * tokens, width), 8, (10**8, 10**6))(give, back))
    far = swapped(call(half_kernel, bf16(tokens, width), 4, (10**6, 10**6))(parts))
    out = call(total_kernel, bf16(tokens, width), 4, (10**6, 10**6))(parts, far)
    return out[None]


def solution(mesh):
    split = Mesh(mesh.devices.reshape(-1, YS, ZS // QUAD, QUAD), ("section", "y", "zh", "zl"))
    line = ("y", "zh", "zl")
    over = P("section", line, None)
    weight = P(line, None, None)
    in_specs = (over, over, over, P("section", line, None, None), weight, weight, weight)
    return jax.shard_map(body, mesh=split, in_specs=in_specs, out_specs=over, check_vma=False)
```

```python
import jax
import jax.numpy as jnp
from jax import lax
from jax.experimental import pallas as pl
from jax.experimental.pallas import tpu as pltpu
from jax.sharding import Mesh, PartitionSpec as P

BF = jnp.bfloat16
F32 = jnp.float32
YS = 4
ZS = 8
QUAD = 4
LANES = 128
MIB = 1 << 20
PARTS = 2


def call(kernel, outs, limit, cost):
    return pl.pallas_call(
        kernel,
        out_shape=outs,
        compiler_params=pltpu.CompilerParams(vmem_limit_bytes=limit * MIB),
        cost_estimate=pl.CostEstimate(flops=cost[0], bytes_accessed=cost[1], transcendentals=0),
    )


def bf16(*shape):
    return jax.ShapeDtypeStruct(shape, BF)


def iota(shape, dim):
    return lax.broadcasted_iota(jnp.int32, shape, dim)


def dot(a, b, dims=((1,), (0,))):
    return lax.dot_general(a, b, (dims, ((), ())), preferred_element_type=F32)


def flag(mask):
    return jnp.where(mask, 1.0, 0.0).astype(BF)


def shares_kernel(ids_hbm, probs_hbm, out_ref, ids, probs, sems):
    copies = [
        pltpu.make_async_copy(src, dst, sems.at[k])
        for k, (src, dst) in enumerate(((ids_hbm, ids), (probs_hbm, probs)))
    ]
    for copy in copies:
        copy.start()
    for copy in copies:
        copy.wait()
    tokens, lanes = out_ref.shape
    expert = iota((lanes, tokens), 0)
    acc = jnp.zeros((lanes, tokens), F32)
    for k in range(ids.shape[0]):
        acc = acc + jnp.where(ids[k : k + 1, :] == expert, probs[k : k + 1, :].astype(F32), 0.0)
    eye = flag(iota((tokens, tokens), 0) == iota((tokens, tokens), 1))
    out_ref[...] = dot(eye, acc.astype(BF), ((1,), (1,))).astype(BF)


def payload_kernel(near_ref, far_ref, near_share_ref, far_share_ref, out_ref):
    own, width = near_ref.shape
    for k in range(QUAD):
        out_ref[k, :own, :width] = near_ref[...]
        out_ref[k, own:, :width] = far_ref[...]
        out_ref[k, :own, width:] = near_share_ref[...]
        out_ref[k, own:, width:] = far_share_ref[...]


def pack_kernel(cap, own, rows_ref, sent_ref, give_ref):
    _, slots, toks = give_ref.shape
    width = sent_ref.shape[3]
    mine = lax.axis_index("zh")
    z = mine * QUAD + lax.axis_index("zl")
    r = iota((slots, LANES), 0)
    wanted = flag((r // (cap * QUAD)) * ZS + z == iota((slots, LANES), 1))
    i, j = iota((toks, toks), 0), iota((toks, toks), 1)
    before = flag((i < j) & (i // own == j // own))
    rr, tt = iota((slots, toks), 0), iota((slots, toks), 1)
    for k in range(2):
        rows = rows_ref[:, k * own : (k + 1) * own, :].reshape(toks, -1)
        share_at = dot(wanted, rows[:, width:], ((1,), (1,)))
        earlier = dot(flag(share_at > 0), before)
        hit = (share_at > 0) & (tt // own == (rr // cap) % QUAD) & (earlier == (rr % cap).astype(F32))
        give_ref[k] = jnp.where(hit, share_at, 0.0).astype(BF)
        packed = dot(flag(hit), rows[:, :width]).astype(BF)
        sent_ref[:, pl.ds((mine + k) % 2, 1)] = packed.reshape(YS, 1, slots // YS, width)


def combine_kernel(give_ref, rows_ref, near_ref, far_ref):
    mine = lax.axis_index("zh")
    slots = give_ref.shape[1]
    for k, out_ref in ((1, far_ref), (0, near_ref)):
        rows = rows_ref[:, pl.ds((mine + k) % 2, 1)].reshape(slots, -1)
        out_ref[...] = dot(give_ref[k], rows, ((0,), (0,))).astype(BF)


def expert_kernel(rows_ref, kept_ref, gate_ref, up_hbm, down_hbm, out_ref, up, down, hidden, sems):
    ff, width = down.shape
    parts = sems.shape[0] // 2
    begun = []
    for src, dst in ((down_hbm, down), (up_hbm, up)):
        step = src.shape[0] // parts
        for k in range(parts):
            at = pl.ds(k * step, step)
            copy = pltpu.make_async_copy(src.at[at], dst.at[at], sems.at[len(begun)])
            copy.start()
            begun.append((copy, at))
    for copy, at in begun[:parts]:
        copy.wait()
        hidden[:, at] = dot(rows_ref[...], down[at, :], ((1,), (1,)))
    h = hidden[...]
    g = kept_ref[:, :ff].astype(F32)
    u = kept_ref[:, ff:].astype(F32)
    s = jax.nn.sigmoid(g)
    hs = h * s
    up_grad = (hs * g).astype(BF)
    gate_grad = (hs * u * (1.0 + g * (1.0 - s))).astype(BF)
    for copy, at in begun[parts:]:
        copy.wait()
        total = dot(gate_grad, gate_ref[at, :], ((1,), (1,))) + dot(up_grad, up[at, :], ((1,), (1,)))
        out_ref[:, at] = total.astype(BF)


def sum_of(parts_ref):
    acc = parts_ref[0].astype(F32)
    for k in range(1, parts_ref.shape[0]):
        acc = acc + parts_ref[k].astype(F32)
    return acc


def half_kernel(parts_ref, out_ref):
    out_ref[...] = sum_of(parts_ref).astype(BF)


def total_kernel(parts_ref, far_ref, out_ref):
    out_ref[...] = (sum_of(parts_ref) + far_ref[...].astype(F32)).astype(BF)


def swapped(x):
    return lax.ppermute(x, "zh", [(0, 1), (1, 0)])


def quad(x):
    return lax.all_to_all(x, "zl", 0, 0, tiled=True)


def across(x):
    return lax.all_to_all(x.reshape(YS, -1, x.shape[-1]), "y", 0, 0, tiled=True).reshape(x.shape)


def body(cotangent, expert_ids, gate_probs, saved, w_gate, w_up, w_down):
    sections = lax.axis_size("section")
    tokens, width = cotangent.shape[1:]
    slots = saved.shape[2]
    cap = slots // (YS * ZS)
    half = QUAD * tokens
    halves = ZS // QUAD
    moves = [
        ((q * halves + h) * QUAD + k, ((q - 1) % sections * halves + (h + 1) % halves) * QUAD + k)
        for q in range(sections)
        for h in range(halves)
        for k in range(QUAD)
    ]
    shares = pl.pallas_call(
        shares_kernel,
        out_shape=bf16(tokens, LANES),
        in_specs=[pl.BlockSpec(memory_space=pl.ANY)] * 2,
        scratch_shapes=[
            pltpu.VMEM((expert_ids.shape[2], tokens), jnp.int32),
            pltpu.VMEM((expert_ids.shape[2], tokens), BF),
            pltpu.SemaphoreType.DMA((2,)),
        ],
        compiler_params=pltpu.CompilerParams(vmem_limit_bytes=58 * MIB),
        cost_estimate=pl.CostEstimate(flops=10**5, bytes_accessed=10**4, transcendentals=0),
    )(expert_ids[0].T, gate_probs[0].T)
    far_shares, cotangent = lax.optimization_barrier((swapped(shares), cotangent))
    crossed = lax.ppermute(cotangent[0], ("section", "zh", "zl"), moves)
    incoming = lax.ppermute(cotangent[0], "section", [(i, (i - 1) % sections) for i in range(sections)])
    payload = call(payload_kernel, bf16(QUAD, 2 * tokens, width + LANES), 4, (10**5, 10**6))(
        incoming, crossed, shares, far_shares
    )
    sent, give = call(
        lambda *refs: pack_kernel(cap, tokens, *refs),
        (bf16(YS, 2, slots // (2 * YS), width), bf16(2, slots // 2, half)),
        8,
        (10**8, 10**6),
    )(quad(payload))
    vm = pl.BlockSpec(memory_space=pltpu.VMEM)
    anywhere = pl.BlockSpec(memory_space=pl.ANY)
    grads = pl.pallas_call(
        expert_kernel,
        out_shape=bf16(slots, width),
        in_specs=[vm, vm, vm, anywhere, anywhere],
        out_specs=vm,
        scratch_shapes=[
            pltpu.VMEM(w_up.shape[1:], BF),
            pltpu.VMEM(w_down.shape[1:], BF),
            pltpu.VMEM((slots, w_down.shape[1]), F32),
            pltpu.SemaphoreType.DMA((2 * PARTS,)),
        ],
        compiler_params=pltpu.CompilerParams(vmem_limit_bytes=48 * MIB),
        cost_estimate=pl.CostEstimate(flops=24 * 10**8, bytes_accessed=12 * 10**6, transcendentals=0),
    )(across(sent).reshape(slots, width), saved[0, 0], w_gate[0], w_up[0], w_down[0])
    back = across(grads).reshape(sent.shape)
    near, far = call(combine_kernel, (bf16(half, width), bf16(half, width)), 8, (10**8, 10**6))(give, back)
    far = quad(far.reshape(QUAD, tokens, width))
    far = swapped(call(half_kernel, bf16(tokens, width), 4, (10**6, 10**6))(far))
    near = quad(near.reshape(QUAD, tokens, width))
    out = call(total_kernel, bf16(tokens, width), 4, (10**6, 10**6))(near, far)
    return out[None]


def solution(mesh):
    split = Mesh(mesh.devices.reshape(-1, YS, ZS // QUAD, QUAD), ("section", "y", "zh", "zl"))
    line = ("y", "zh", "zl")
    over = P("section", line, None)
    weight = P(line, None, None)
    in_specs = (over, over, over, P("section", line, None, None), weight, weight, weight)
    return jax.shard_map(body, mesh=split, in_specs=in_specs, out_specs=over, check_vma=False)
```

```python
import jax
import jax.numpy as jnp
from jax import lax
from jax.experimental import pallas as pl
from jax.experimental.pallas import tpu as pltpu
from jax.sharding import Mesh, PartitionSpec as P

BF = jnp.bfloat16
F32 = jnp.float32
YS = 4
ZS = 8
QUAD = 4
LANES = 128
MIB = 1 << 20
PARTS = 2


def call(kernel, outs, limit, cost):
    return pl.pallas_call(
        kernel,
        out_shape=outs,
        compiler_params=pltpu.CompilerParams(vmem_limit_bytes=limit * MIB),
        cost_estimate=pl.CostEstimate(flops=cost[0], bytes_accessed=cost[1], transcendentals=0),
    )


def bf16(*shape):
    return jax.ShapeDtypeStruct(shape, BF)


def iota(shape, dim):
    return lax.broadcasted_iota(jnp.int32, shape, dim)


def dot(a, b, dims=((1,), (0,))):
    return lax.dot_general(a, b, (dims, ((), ())), preferred_element_type=F32)


def flag(mask):
    return jnp.where(mask, 1.0, 0.0).astype(BF)


def shares_kernel(ids_ref, probs_ref, out_ref):
    shape = out_ref.shape
    expert = iota(shape, 1)
    acc = jnp.zeros(shape, F32)
    for k in range(ids_ref.shape[1]):
        acc = acc + jnp.where(ids_ref[:, k : k + 1] == expert, probs_ref[:, k : k + 1].astype(F32), 0.0)
    out_ref[...] = acc.astype(BF)


def payload_kernel(rows_ref, share_ref, out_ref):
    width = rows_ref.shape[1]
    for k in range(ZS):
        out_ref[k, :, :width] = rows_ref[...]
        out_ref[k, :, width:] = share_ref[...]


def pack_kernel(cap, own, rows_ref, sent_ref, give_ref):
    _, slots, toks = give_ref.shape
    width = sent_ref.shape[3]
    mine = lax.axis_index("zh")
    z = mine * QUAD + lax.axis_index("zl")
    r = iota((slots, LANES), 0)
    wanted = flag((r // (cap * QUAD)) * ZS + z == iota((slots, LANES), 1))
    i, j = iota((toks, toks), 0), iota((toks, toks), 1)
    before = flag((i < j) & (i // own == j // own))
    rr, tt = iota((slots, toks), 0), iota((slots, toks), 1)
    for k in range(2):
        rows = rows_ref[pl.ds((mine + k) % 2 * QUAD, QUAD)].reshape(toks, -1)
        share_at = dot(wanted, rows[:, width:], ((1,), (1,)))
        earlier = dot(flag(share_at > 0), before)
        hit = (share_at > 0) & (tt // own == (rr // cap) % QUAD) & (earlier == (rr % cap).astype(F32))
        give_ref[k] = jnp.where(hit, share_at, 0.0).astype(BF)
        packed = dot(flag(hit), rows[:, :width]).astype(BF)
        sent_ref[:, pl.ds((mine + k) % 2, 1)] = packed.reshape(YS, 1, slots // YS, width)


def combine_kernel(give_ref, rows_ref, near_ref, far_ref):
    mine = lax.axis_index("zh")
    slots = give_ref.shape[1]
    for k, out_ref in ((1, far_ref), (0, near_ref)):
        rows = rows_ref[:, pl.ds((mine + k) % 2, 1)].reshape(slots, -1)
        out_ref[...] = dot(give_ref[k], rows, ((0,), (0,))).astype(BF)


def expert_kernel(rows_ref, kept_ref, gate_ref, up_hbm, down_hbm, out_ref, up, down, hidden, sems):
    ff, width = down.shape
    parts = sems.shape[0] // 2
    begun = []
    for src, dst in ((down_hbm, down), (up_hbm, up)):
        step = src.shape[0] // parts
        for k in range(parts):
            at = pl.ds(k * step, step)
            copy = pltpu.make_async_copy(src.at[at], dst.at[at], sems.at[len(begun)])
            copy.start()
            begun.append((copy, at))
    for copy, at in begun[:parts]:
        copy.wait()
        hidden[:, at] = dot(rows_ref[...], down[at, :], ((1,), (1,)))
    h = hidden[...]
    g = kept_ref[:, :ff].astype(F32)
    u = kept_ref[:, ff:].astype(F32)
    s = jax.nn.sigmoid(g)
    hs = h * s
    up_grad = (hs * g).astype(BF)
    gate_grad = (hs * u * (1.0 + g * (1.0 - s))).astype(BF)
    for copy, at in begun[parts:]:
        copy.wait()
        total = dot(gate_grad, gate_ref[at, :], ((1,), (1,))) + dot(up_grad, up[at, :], ((1,), (1,)))
        out_ref[:, at] = total.astype(BF)


def sum_of(parts_ref):
    acc = parts_ref[0].astype(F32)
    for k in range(1, parts_ref.shape[0]):
        acc = acc + parts_ref[k].astype(F32)
    return acc


def half_kernel(parts_ref, out_ref):
    out_ref[...] = sum_of(parts_ref).astype(BF)


def total_kernel(parts_ref, far_ref, out_ref):
    out_ref[...] = (sum_of(parts_ref) + far_ref[...].astype(F32)).astype(BF)


def swapped(x):
    return lax.ppermute(x, "zh", [(0, 1), (1, 0)])


def quad(x):
    return lax.all_to_all(x, "zl", 0, 0, tiled=True)


def across(x):
    return lax.all_to_all(x.reshape(YS, -1, x.shape[-1]), "y", 0, 0, tiled=True).reshape(x.shape)


def body(cotangent, expert_ids, gate_probs, saved, w_gate, w_up, w_down):
    sections = lax.axis_size("section")
    tokens, width = cotangent.shape[1:]
    slots = saved.shape[2]
    cap = slots // (YS * ZS)
    half = QUAD * tokens
    incoming = lax.ppermute(cotangent[0], "section", [(i, (i - 1) % sections) for i in range(sections)])
    shares = call(shares_kernel, bf16(tokens, LANES), 4, (10**5, 10**4))(expert_ids[0], gate_probs[0])
    payload = call(payload_kernel, bf16(ZS, tokens, width + LANES), 4, (10**5, 10**6))(incoming, shares)
    gathered = lax.all_to_all(payload, ("zh", "zl"), 0, 0, tiled=True)
    sent, give = call(
        lambda *refs: pack_kernel(cap, tokens, *refs),
        (bf16(YS, 2, slots // (2 * YS), width), bf16(2, slots // 2, half)),
        8,
        (10**8, 10**6),
    )(gathered)
    vm = pl.BlockSpec(memory_space=pltpu.VMEM)
    anywhere = pl.BlockSpec(memory_space=pl.ANY)
    grads = pl.pallas_call(
        expert_kernel,
        out_shape=bf16(slots, width),
        in_specs=[vm, vm, vm, anywhere, anywhere],
        out_specs=vm,
        scratch_shapes=[
            pltpu.VMEM(w_up.shape[1:], BF),
            pltpu.VMEM(w_down.shape[1:], BF),
            pltpu.VMEM((slots, w_down.shape[1]), F32),
            pltpu.SemaphoreType.DMA((2 * PARTS,)),
        ],
        compiler_params=pltpu.CompilerParams(vmem_limit_bytes=48 * MIB),
        cost_estimate=pl.CostEstimate(flops=24 * 10**8, bytes_accessed=12 * 10**6, transcendentals=0),
    )(across(sent).reshape(slots, width), saved[0, 0], w_gate[0], w_up[0], w_down[0])
    back = across(grads).reshape(sent.shape)
    near, far = call(combine_kernel, (bf16(half, width), bf16(half, width)), 8, (10**8, 10**6))(give, back)
    far = quad(far.reshape(QUAD, tokens, width))
    far = swapped(call(half_kernel, bf16(tokens, width), 4, (10**6, 10**6))(far))
    near = quad(near.reshape(QUAD, tokens, width))
    out = call(total_kernel, bf16(tokens, width), 4, (10**6, 10**6))(near, far)
    return out[None]


def solution(mesh):
    split = Mesh(mesh.devices.reshape(-1, YS, ZS // QUAD, QUAD), ("section", "y", "zh", "zl"))
    line = ("y", "zh", "zl")
    over = P("section", line, None)
    weight = P(line, None, None)
    in_specs = (over, over, over, P("section", line, None, None), weight, weight, weight)
    return jax.shard_map(body, mesh=split, in_specs=in_specs, out_specs=over, check_vma=False)
```

```python
import jax
import jax.numpy as jnp
from jax import lax
from jax.experimental import pallas as pl
from jax.experimental.pallas import tpu as pltpu
from jax.sharding import Mesh, PartitionSpec as P

BF = jnp.bfloat16
F32 = jnp.float32
YS = 4
ZS = 8
QUAD = 4
LANES = 128
MIB = 1 << 20
PARTS = 2


def call(kernel, outs, limit, cost):
    return pl.pallas_call(
        kernel,
        out_shape=outs,
        compiler_params=pltpu.CompilerParams(vmem_limit_bytes=limit * MIB),
        cost_estimate=pl.CostEstimate(flops=cost[0], bytes_accessed=cost[1], transcendentals=0),
    )


def bf16(*shape):
    return jax.ShapeDtypeStruct(shape, BF)


def iota(shape, dim):
    return lax.broadcasted_iota(jnp.int32, shape, dim)


def dot(a, b, dims=((1,), (0,))):
    return lax.dot_general(a, b, (dims, ((), ())), preferred_element_type=F32)


def flag(mask):
    return jnp.where(mask, 1.0, 0.0).astype(BF)


def shares_kernel(ids_hbm, probs_hbm, out_ref, ids, probs, sems):
    copies = [
        pltpu.make_async_copy(src, dst, sems.at[k])
        for k, (src, dst) in enumerate(((ids_hbm, ids), (probs_hbm, probs)))
    ]
    for copy in copies:
        copy.start()
    for copy in copies:
        copy.wait()
    tokens, lanes = out_ref.shape
    expert = iota((lanes, tokens), 0)
    acc = jnp.zeros((lanes, tokens), F32)
    for k in range(ids.shape[0]):
        acc = acc + jnp.where(ids[k : k + 1, :] == expert, probs[k : k + 1, :].astype(F32), 0.0)
    eye = flag(iota((tokens, tokens), 0) == iota((tokens, tokens), 1))
    out_ref[...] = dot(eye, acc.astype(BF), ((1,), (1,))).astype(BF)


def payload_kernel(near_ref, far_ref, near_share_ref, early_ref, late_ref, out_ref):
    own, width = near_ref.shape
    far_share = early_ref[...] + late_ref[...]
    for k in range(QUAD):
        out_ref[k, :own, :width] = near_ref[...]
        out_ref[k, own:, :width] = far_ref[...]
        out_ref[k, :own, width:] = near_share_ref[...]
        out_ref[k, own:, width:] = far_share


def pack_kernel(cap, own, rows_ref, sent_ref, give_ref):
    _, slots, toks = give_ref.shape
    width = sent_ref.shape[3]
    mine = lax.axis_index("zh")
    z = mine * QUAD + lax.axis_index("zl")
    r = iota((slots, LANES), 0)
    wanted = flag((r // (cap * QUAD)) * ZS + z == iota((slots, LANES), 1))
    i, j = iota((toks, toks), 0), iota((toks, toks), 1)
    before = flag((i < j) & (i // own == j // own))
    rr, tt = iota((slots, toks), 0), iota((slots, toks), 1)
    for k in range(2):
        rows = rows_ref[:, k * own : (k + 1) * own, :].reshape(toks, -1)
        share_at = dot(wanted, rows[:, width:], ((1,), (1,)))
        earlier = dot(flag(share_at > 0), before)
        hit = (share_at > 0) & (tt // own == (rr // cap) % QUAD) & (earlier == (rr % cap).astype(F32))
        give_ref[k] = jnp.where(hit, share_at, 0.0).astype(BF)
        packed = dot(flag(hit), rows[:, :width]).astype(BF)
        sent_ref[:, pl.ds((mine + k) % 2, 1)] = packed.reshape(YS, 1, slots // YS, width)


def combine_kernel(give_ref, rows_ref, near_ref, far_ref):
    mine = lax.axis_index("zh")
    slots = give_ref.shape[1]
    for k, out_ref in ((1, far_ref), (0, near_ref)):
        rows = rows_ref[:, pl.ds((mine + k) % 2, 1)].reshape(slots, -1)
        out_ref[...] = dot(give_ref[k], rows, ((0,), (0,))).astype(BF)


def expert_kernel(rows_ref, kept_ref, gate_ref, up_hbm, down_hbm, out_ref, up, down, hidden, sems):
    ff, width = down.shape
    parts = sems.shape[0] // 2
    begun = []
    for src, dst in ((down_hbm, down), (up_hbm, up)):
        step = src.shape[0] // parts
        for k in range(parts):
            at = pl.ds(k * step, step)
            copy = pltpu.make_async_copy(src.at[at], dst.at[at], sems.at[len(begun)])
            begun.append((copy, at))
    for copy, at in begun[:parts]:
        copy.start()
    for k, (copy, at) in enumerate(begun[:parts]):
        copy.wait()
        if k == 0:
            for later, _ in begun[parts:]:
                later.start()
        hidden[:, at] = dot(rows_ref[...], down[at, :], ((1,), (1,)))
    h = hidden[...]
    g = kept_ref[:, :ff].astype(F32)
    u = kept_ref[:, ff:].astype(F32)
    s = jax.nn.sigmoid(g)
    hs = h * s
    up_grad = (hs * g).astype(BF)
    gate_grad = (hs * u * (1.0 + g * (1.0 - s))).astype(BF)
    for copy, at in begun[parts:]:
        copy.wait()
        total = dot(gate_grad, gate_ref[at, :], ((1,), (1,))) + dot(up_grad, up[at, :], ((1,), (1,)))
        out_ref[:, at] = total.astype(BF)


def sum_of(parts_ref):
    acc = parts_ref[0].astype(F32)
    for k in range(1, parts_ref.shape[0]):
        acc = acc + parts_ref[k].astype(F32)
    return acc


def half_kernel(parts_ref, out_ref):
    out_ref[...] = sum_of(parts_ref).astype(BF)


def total_kernel(parts_ref, far_ref, out_ref):
    out_ref[...] = (sum_of(parts_ref) + far_ref[...].astype(F32)).astype(BF)


def swapped(x):
    return lax.ppermute(x, "zh", [(0, 1), (1, 0)])


def quad(x):
    return lax.all_to_all(x, "zl", 0, 0, tiled=True)


def across(x):
    return lax.all_to_all(x.reshape(YS, -1, x.shape[-1]), "y", 0, 0, tiled=True).reshape(x.shape)


def body(cotangent, expert_ids, gate_probs, saved, w_gate, w_up, w_down):
    sections = lax.axis_size("section")
    tokens, width = cotangent.shape[1:]
    slots = saved.shape[2]
    cap = slots // (YS * ZS)
    half = QUAD * tokens
    halves = ZS // QUAD
    moves = [
        ((q * halves + h) * QUAD + k, ((q - 1) % sections * halves + (h + 1) % halves) * QUAD + k)
        for q in range(sections)
        for h in range(halves)
        for k in range(QUAD)
    ]
    shares = pl.pallas_call(
        shares_kernel,
        out_shape=bf16(tokens, LANES),
        in_specs=[pl.BlockSpec(memory_space=pl.ANY)] * 2,
        scratch_shapes=[
            pltpu.VMEM((expert_ids.shape[2], tokens), jnp.int32),
            pltpu.VMEM((expert_ids.shape[2], tokens), BF),
            pltpu.SemaphoreType.DMA((2,)),
        ],
        compiler_params=pltpu.CompilerParams(vmem_limit_bytes=58 * MIB),
        cost_estimate=pl.CostEstimate(flops=10**5, bytes_accessed=10**4, transcendentals=0),
    )(expert_ids[0].T, gate_probs[0].T)
    early, late = (
        [(q * halves + h, q * halves + (h + 1) % halves) for q in range(first, sections, 2) for h in range(halves)]
        for first in (0, 1)
    )
    early_shares, cotangent = lax.optimization_barrier((lax.ppermute(shares, ("section", "zh"), early), cotangent))
    late_shares = lax.ppermute(shares, ("section", "zh"), late)
    crossed = lax.ppermute(cotangent[0], ("section", "zh", "zl"), moves)
    incoming = lax.ppermute(cotangent[0], "section", [(i, (i - 1) % sections) for i in range(sections)])
    payload = call(payload_kernel, bf16(QUAD, 2 * tokens, width + LANES), 4, (10**5, 10**6))(
        incoming, crossed, shares, early_shares, late_shares
    )
    sent, give = call(
        lambda *refs: pack_kernel(cap, tokens, *refs),
        (bf16(YS, 2, slots // (2 * YS), width), bf16(2, slots // 2, half)),
        8,
        (10**8, 10**6),
    )(quad(payload))
    vm = pl.BlockSpec(memory_space=pltpu.VMEM)
    anywhere = pl.BlockSpec(memory_space=pl.ANY)
    grads = pl.pallas_call(
        expert_kernel,
        out_shape=bf16(slots, width),
        in_specs=[vm, vm, vm, anywhere, anywhere],
        out_specs=vm,
        scratch_shapes=[
            pltpu.VMEM(w_up.shape[1:], BF),
            pltpu.VMEM(w_down.shape[1:], BF),
            pltpu.VMEM((slots, w_down.shape[1]), F32),
            pltpu.SemaphoreType.DMA((2 * PARTS,)),
        ],
        compiler_params=pltpu.CompilerParams(vmem_limit_bytes=48 * MIB),
        cost_estimate=pl.CostEstimate(flops=24 * 10**8, bytes_accessed=12 * 10**6, transcendentals=0),
    )(across(sent).reshape(slots, width), saved[0, 0], w_gate[0], w_up[0], w_down[0])
    back = across(grads).reshape(sent.shape)
    near, far = call(combine_kernel, (bf16(half, width), bf16(half, width)), 8, (10**8, 10**6))(give, back)
    far = quad(far.reshape(QUAD, tokens, width))
    far = swapped(call(half_kernel, bf16(tokens, width), 4, (10**6, 10**6))(far))
    near = quad(near.reshape(QUAD, tokens, width))
    out = call(total_kernel, bf16(tokens, width), 4, (10**6, 10**6))(near, far)
    return out[None]


def solution(mesh):
    split = Mesh(mesh.devices.reshape(-1, YS, ZS // QUAD, QUAD), ("section", "y", "zh", "zl"))
    line = ("y", "zh", "zl")
    over = P("section", line, None)
    weight = P(line, None, None)
    in_specs = (over, over, over, P("section", line, None, None), weight, weight, weight)
    return jax.shard_map(body, mesh=split, in_specs=in_specs, out_specs=over, check_vma=False)
```

```python
import jax
import jax.numpy as jnp
from jax import lax
from jax.experimental import pallas as pl
from jax.experimental.pallas import tpu as pltpu
from jax.sharding import Mesh, PartitionSpec as P

BF = jnp.bfloat16
F32 = jnp.float32
YS = 4
ZS = 8
QUAD = 4
LANES = 128
MIB = 1 << 20
DOWN_PARTS = 3
UP_PARTS = 4


def call(kernel, outs, limit, cost):
    return pl.pallas_call(
        kernel,
        out_shape=outs,
        compiler_params=pltpu.CompilerParams(vmem_limit_bytes=limit * MIB),
        cost_estimate=pl.CostEstimate(flops=cost[0], bytes_accessed=cost[1], transcendentals=0),
    )


def bf16(*shape):
    return jax.ShapeDtypeStruct(shape, BF)


def iota(shape, dim):
    return lax.broadcasted_iota(jnp.int32, shape, dim)


def dot(a, b, dims=((1,), (0,))):
    return lax.dot_general(a, b, (dims, ((), ())), preferred_element_type=F32)


def flag(mask):
    return jnp.where(mask, 1.0, 0.0).astype(BF)


def shares_kernel(ids_ref, probs_ref, out_ref):
    shape = out_ref.shape
    expert = iota(shape, 1)
    acc = jnp.zeros(shape, F32)
    for k in range(ids_ref.shape[1]):
        acc = acc + jnp.where(ids_ref[:, k : k + 1] == expert, probs_ref[:, k : k + 1].astype(F32), 0.0)
    out_ref[...] = acc.astype(BF)


def payload_kernel(rows_ref, share_ref, out_ref):
    width = rows_ref.shape[1]
    out_ref[:, :width] = rows_ref[...]
    out_ref[:, width:] = share_ref[...]


def copies_kernel(near_ref, far_ref, out_ref):
    own = near_ref.shape[0]
    for k in range(QUAD):
        out_ref[k, :own] = near_ref[...]
        out_ref[k, own:] = far_ref[...]


def pack_kernel(cap, own, rows_ref, sent_ref, give_ref):
    _, slots, toks = give_ref.shape
    width = sent_ref.shape[3]
    mine = lax.axis_index("zh")
    z = mine * QUAD + lax.axis_index("zl")
    r = iota((slots, LANES), 0)
    wanted = flag((r // (cap * QUAD)) * ZS + z == iota((slots, LANES), 1))
    i, j = iota((toks, toks), 0), iota((toks, toks), 1)
    before = flag((i < j) & (i // own == j // own))
    rr, tt = iota((slots, toks), 0), iota((slots, toks), 1)
    for k in range(2):
        rows = rows_ref[:, k * own : (k + 1) * own, :].reshape(toks, -1)
        share_at = dot(wanted, rows[:, width:], ((1,), (1,)))
        earlier = dot(flag(share_at > 0), before)
        hit = (share_at > 0) & (tt // own == (rr // cap) % QUAD) & (earlier == (rr % cap).astype(F32))
        give_ref[k] = jnp.where(hit, share_at, 0.0).astype(BF)
        packed = dot(flag(hit), rows[:, :width]).astype(BF)
        sent_ref[:, pl.ds((mine + k) % 2, 1)] = packed.reshape(YS, 1, slots // YS, width)


def combine_kernel(give_ref, rows_ref, near_ref, far_ref):
    mine = lax.axis_index("zh")
    slots = give_ref.shape[1]
    for k, out_ref in ((1, far_ref), (0, near_ref)):
        rows = rows_ref[:, pl.ds((mine + k) % 2, 1)].reshape(slots, -1)
        out_ref[...] = dot(give_ref[k], rows, ((0,), (0,))).astype(BF)


def expert_kernel(rows_ref, kept_ref, gate_ref, up_hbm, down_hbm, out_ref, up, down, hidden, sems):
    ff, width = down.shape
    begun = []
    for src, dst, parts in ((down_hbm, down, DOWN_PARTS), (up_hbm, up, UP_PARTS)):
        step = src.shape[0] // parts
        for k in range(parts):
            at = pl.ds(k * step, step)
            copy = pltpu.make_async_copy(src.at[at], dst.at[at], sems.at[len(begun)])
            copy.start()
            begun.append((copy, at))
    for copy, at in begun[:DOWN_PARTS]:
        copy.wait()
        hidden[:, at] = dot(rows_ref[...], down[at, :], ((1,), (1,)))
    h = hidden[...]
    g = kept_ref[:, :ff].astype(F32)
    u = kept_ref[:, ff:].astype(F32)
    s = jax.nn.sigmoid(g)
    hs = h * s
    up_grad = (hs * g).astype(BF)
    gate_grad = (hs * u * (1.0 + g * (1.0 - s))).astype(BF)
    for copy, at in begun[DOWN_PARTS:]:
        copy.wait()
        total = dot(gate_grad, gate_ref[at, :], ((1,), (1,))) + dot(up_grad, up[at, :], ((1,), (1,)))
        out_ref[:, at] = total.astype(BF)


def sum_of(parts_ref):
    acc = parts_ref[0].astype(F32)
    for k in range(1, parts_ref.shape[0]):
        acc = acc + parts_ref[k].astype(F32)
    return acc


def half_kernel(parts_ref, out_ref):
    out_ref[...] = sum_of(parts_ref).astype(BF)


def total_kernel(parts_ref, far_ref, out_ref):
    out_ref[...] = (sum_of(parts_ref) + far_ref[...].astype(F32)).astype(BF)


def swapped(x):
    return lax.ppermute(x, "zh", [(0, 1), (1, 0)])


def quad(x):
    return lax.all_to_all(x, "zl", 0, 0, tiled=True)


def across(x):
    return lax.all_to_all(x.reshape(YS, -1, x.shape[-1]), "y", 0, 0, tiled=True).reshape(x.shape)


def body(cotangent, expert_ids, gate_probs, saved, w_gate, w_up, w_down):
    sections = lax.axis_size("section")
    tokens, width = cotangent.shape[1:]
    slots = saved.shape[2]
    cap = slots // (YS * ZS)
    half = QUAD * tokens
    incoming = lax.ppermute(cotangent[0], "section", [(i, (i - 1) % sections) for i in range(sections)])
    shares = call(shares_kernel, bf16(tokens, LANES), 4, (10**5, 10**4))(expert_ids[0], gate_probs[0])
    one = call(payload_kernel, bf16(tokens, width + LANES), 4, (10**5, 10**6))(incoming, shares)
    payload = call(copies_kernel, bf16(QUAD, 2 * tokens, width + LANES), 4, (10**5, 10**6))(one, swapped(one))
    sent, give = call(
        lambda *refs: pack_kernel(cap, tokens, *refs),
        (bf16(YS, 2, slots // (2 * YS), width), bf16(2, slots // 2, half)),
        8,
        (10**8, 10**6),
    )(quad(payload))
    vm = pl.BlockSpec(memory_space=pltpu.VMEM)
    anywhere = pl.BlockSpec(memory_space=pl.ANY)
    grads = pl.pallas_call(
        expert_kernel,
        out_shape=bf16(slots, width),
        in_specs=[vm, vm, vm, anywhere, anywhere],
        out_specs=vm,
        scratch_shapes=[
            pltpu.VMEM(w_up.shape[1:], BF),
            pltpu.VMEM(w_down.shape[1:], BF),
            pltpu.VMEM((slots, w_down.shape[1]), F32),
            pltpu.SemaphoreType.DMA((DOWN_PARTS + UP_PARTS,)),
        ],
        compiler_params=pltpu.CompilerParams(vmem_limit_bytes=48 * MIB),
        cost_estimate=pl.CostEstimate(flops=24 * 10**8, bytes_accessed=12 * 10**6, transcendentals=0),
    )(across(sent).reshape(slots, width), saved[0, 0], w_gate[0], w_up[0], w_down[0])
    back = across(grads).reshape(sent.shape)
    near, far = call(combine_kernel, (bf16(half, width), bf16(half, width)), 8, (10**8, 10**6))(give, back)
    far = quad(far.reshape(QUAD, tokens, width))
    far = swapped(call(half_kernel, bf16(tokens, width), 4, (10**6, 10**6))(far))
    near = quad(near.reshape(QUAD, tokens, width))
    out = call(total_kernel, bf16(tokens, width), 4, (10**6, 10**6))(near, far)
    return out[None]


def solution(mesh):
    split = Mesh(mesh.devices.reshape(-1, YS, ZS // QUAD, QUAD), ("section", "y", "zh", "zl"))
    line = ("y", "zh", "zl")
    over = P("section", line, None)
    weight = P(line, None, None)
    in_specs = (over, over, over, P("section", line, None, None), weight, weight, weight)
    return jax.shard_map(body, mesh=split, in_specs=in_specs, out_specs=over, check_vma=False)
```

```python
import jax
import jax.numpy as jnp
from jax import lax
from jax.experimental import pallas as pl
from jax.experimental.pallas import tpu as pltpu
from jax.sharding import Mesh, PartitionSpec as P

BF = jnp.bfloat16
F32 = jnp.float32
YS = 4
ZS = 8
QUAD = 4
LANES = 128
MIB = 1 << 20
DOWN_PARTS = 2
UP_PARTS = 1


def call(kernel, outs, limit, cost):
    return pl.pallas_call(
        kernel,
        out_shape=outs,
        compiler_params=pltpu.CompilerParams(vmem_limit_bytes=limit * MIB),
        cost_estimate=pl.CostEstimate(flops=cost[0], bytes_accessed=cost[1], transcendentals=0),
    )


def bf16(*shape):
    return jax.ShapeDtypeStruct(shape, BF)


def iota(shape, dim):
    return lax.broadcasted_iota(jnp.int32, shape, dim)


def dot(a, b, dims=((1,), (0,))):
    return lax.dot_general(a, b, (dims, ((), ())), preferred_element_type=F32)


def flag(mask):
    return jnp.where(mask, 1.0, 0.0).astype(BF)


def shares_kernel(ids_ref, probs_ref, out_ref):
    shape = out_ref.shape
    expert = iota(shape, 1)
    acc = jnp.zeros(shape, F32)
    for k in range(ids_ref.shape[1]):
        acc = acc + jnp.where(ids_ref[:, k : k + 1] == expert, probs_ref[:, k : k + 1].astype(F32), 0.0)
    out_ref[...] = acc.astype(BF)


def payload_kernel(rows_ref, share_ref, out_ref):
    width = rows_ref.shape[1]
    out_ref[:, :width] = rows_ref[...]
    out_ref[:, width:] = share_ref[...]


def copies_kernel(near_ref, far_ref, out_ref):
    own = near_ref.shape[0]
    for k in range(QUAD):
        out_ref[k, :own] = near_ref[...]
        out_ref[k, own:] = far_ref[...]


def pack_kernel(cap, own, rows_ref, sent_ref, give_ref):
    _, slots, toks = give_ref.shape
    width = sent_ref.shape[3]
    mine = lax.axis_index("zh")
    z = mine * QUAD + lax.axis_index("zl")
    r = iota((slots, LANES), 0)
    wanted = flag((r // (cap * QUAD)) * ZS + z == iota((slots, LANES), 1))
    i, j = iota((toks, toks), 0), iota((toks, toks), 1)
    before = flag((i < j) & (i // own == j // own))
    rr, tt = iota((slots, toks), 0), iota((slots, toks), 1)
    for k in range(2):
        rows = rows_ref[:, k * own : (k + 1) * own, :].reshape(toks, -1)
        share_at = dot(wanted, rows[:, width:], ((1,), (1,)))
        earlier = dot(flag(share_at > 0), before)
        hit = (share_at > 0) & (tt // own == (rr // cap) % QUAD) & (earlier == (rr % cap).astype(F32))
        give_ref[k] = jnp.where(hit, share_at, 0.0).astype(BF)
        packed = dot(flag(hit), rows[:, :width]).astype(BF)
        sent_ref[:, pl.ds((mine + k) % 2, 1)] = packed.reshape(YS, 1, slots // YS, width)


def combine_kernel(give_ref, rows_ref, out_ref):
    mine = lax.axis_index("zh")
    slots = give_ref.shape[1]
    own = out_ref.shape[1]
    for k in range(2):
        half = (mine + k) % 2
        rows = rows_ref[:, pl.ds(half, 1)].reshape(slots, -1)
        part = dot(give_ref[k], rows, ((0,), (0,))).astype(BF)
        out_ref[pl.ds(half * QUAD, QUAD)] = part.reshape(QUAD, own, -1)


def expert_kernel(rows_ref, kept_ref, gate_ref, up_hbm, down_hbm, out_ref, up, down, hidden, sems):
    ff, width = down.shape
    begun = []
    for src, dst, parts in ((down_hbm, down, DOWN_PARTS), (up_hbm, up, UP_PARTS)):
        step = src.shape[0] // parts
        for k in range(parts):
            at = pl.ds(k * step, step)
            copy = pltpu.make_async_copy(src.at[at], dst.at[at], sems.at[len(begun)])
            copy.start()
            begun.append((copy, at))
    for copy, at in begun[:DOWN_PARTS]:
        copy.wait()
        hidden[:, at] = dot(rows_ref[...], down[at, :], ((1,), (1,)))
    h = hidden[...]
    g = kept_ref[:, :ff].astype(F32)
    u = kept_ref[:, ff:].astype(F32)
    s = jax.nn.sigmoid(g)
    hs = h * s
    up_grad = (hs * g).astype(BF)
    gate_grad = (hs * u * (1.0 + g * (1.0 - s))).astype(BF)
    for copy, at in begun[DOWN_PARTS:]:
        copy.wait()
        total = dot(gate_grad, gate_ref[at, :], ((1,), (1,))) + dot(up_grad, up[at, :], ((1,), (1,)))
        out_ref[:, at] = total.astype(BF)


def total_kernel(parts_ref, out_ref):
    acc = parts_ref[0].astype(F32)
    for k in range(1, parts_ref.shape[0]):
        acc = acc + parts_ref[k].astype(F32)
    out_ref[...] = acc.astype(BF)


def swapped(x):
    return lax.ppermute(x, "zh", [(0, 1), (1, 0)])


def quad(x):
    return lax.all_to_all(x, "zl", 0, 0, tiled=True)


def across(x):
    return lax.all_to_all(x.reshape(YS, -1, x.shape[-1]), "y", 0, 0, tiled=True).reshape(x.shape)


def body(cotangent, expert_ids, gate_probs, saved, w_gate, w_up, w_down):
    sections = lax.axis_size("section")
    tokens, width = cotangent.shape[1:]
    slots = saved.shape[2]
    cap = slots // (YS * ZS)
    half = QUAD * tokens
    incoming = lax.ppermute(cotangent[0], "section", [(i, (i - 1) % sections) for i in range(sections)])
    shares = call(shares_kernel, bf16(tokens, LANES), 4, (10**5, 10**4))(expert_ids[0], gate_probs[0])
    one = call(payload_kernel, bf16(tokens, width + LANES), 4, (10**5, 10**6))(incoming, shares)
    payload = call(copies_kernel, bf16(QUAD, 2 * tokens, width + LANES), 4, (10**5, 10**6))(one, swapped(one))
    sent, give = call(
        lambda *refs: pack_kernel(cap, tokens, *refs),
        (bf16(YS, 2, slots // (2 * YS), width), bf16(2, slots // 2, half)),
        8,
        (10**8, 10**6),
    )(quad(payload))
    vm = pl.BlockSpec(memory_space=pltpu.VMEM)
    anywhere = pl.BlockSpec(memory_space=pl.ANY)
    grads = pl.pallas_call(
        expert_kernel,
        out_shape=bf16(slots, width),
        in_specs=[vm, vm, vm, anywhere, anywhere],
        out_specs=vm,
        scratch_shapes=[
            pltpu.VMEM(w_up.shape[1:], BF),
            pltpu.VMEM(w_down.shape[1:], BF),
            pltpu.VMEM((slots, w_down.shape[1]), F32),
            pltpu.SemaphoreType.DMA((DOWN_PARTS + UP_PARTS,)),
        ],
        compiler_params=pltpu.CompilerParams(vmem_limit_bytes=48 * MIB),
        cost_estimate=pl.CostEstimate(flops=24 * 10**8, bytes_accessed=12 * 10**6, transcendentals=0),
    )(across(sent).reshape(slots, width), saved[0, 0], w_gate[0], w_up[0], w_down[0])
    back = across(grads).reshape(sent.shape)
    parts = call(combine_kernel, bf16(ZS, tokens, width), 8, (10**8, 10**6))(give, back)
    parts = lax.all_to_all(parts, ("zh", "zl"), 0, 0, tiled=True)
    out = call(total_kernel, bf16(tokens, width), 4, (10**6, 10**6))(parts)
    return out[None]


def solution(mesh):
    split = Mesh(mesh.devices.reshape(-1, YS, ZS // QUAD, QUAD), ("section", "y", "zh", "zl"))
    line = ("y", "zh", "zl")
    over = P("section", line, None)
    weight = P(line, None, None)
    in_specs = (over, over, over, P("section", line, None, None), weight, weight, weight)
    return jax.shard_map(body, mesh=split, in_specs=in_specs, out_specs=over, check_vma=False)
```

```python
import jax
import jax.numpy as jnp
from jax import lax
from jax.experimental import pallas as pl
from jax.experimental.pallas import tpu as pltpu
from jax.sharding import Mesh, PartitionSpec as P

BF = jnp.bfloat16
F32 = jnp.float32
YS = 4
ZS = 8
QUAD = 4
LANES = 128
MIB = 1 << 20
DOWN_PARTS = 2
UP_PARTS = 1


def call(kernel, outs, limit, cost):
    return pl.pallas_call(
        kernel,
        out_shape=outs,
        compiler_params=pltpu.CompilerParams(vmem_limit_bytes=limit * MIB),
        cost_estimate=pl.CostEstimate(flops=cost[0], bytes_accessed=cost[1], transcendentals=0),
    )


def bf16(*shape):
    return jax.ShapeDtypeStruct(shape, BF)


def iota(shape, dim):
    return lax.broadcasted_iota(jnp.int32, shape, dim)


def dot(a, b, dims=((1,), (0,))):
    return lax.dot_general(a, b, (dims, ((), ())), preferred_element_type=F32)


def flag(mask):
    return jnp.where(mask, 1.0, 0.0).astype(BF)


def shares_kernel(ids_ref, probs_ref, out_ref):
    shape = out_ref.shape
    expert = iota(shape, 1)
    acc = jnp.zeros(shape, F32)
    for k in range(ids_ref.shape[1]):
        acc = acc + jnp.where(ids_ref[:, k : k + 1] == expert, probs_ref[:, k : k + 1].astype(F32), 0.0)
    out_ref[...] = acc.astype(BF)


def payload_kernel(rows_ref, share_ref, out_ref):
    width = rows_ref.shape[1]
    out_ref[:, :width] = rows_ref[...]
    out_ref[:, width:] = share_ref[...]


def copies_kernel(near_ref, far_ref, out_ref):
    own = near_ref.shape[0]
    for k in range(QUAD):
        out_ref[k, :own] = near_ref[...]
        out_ref[k, own:] = far_ref[...]


def pack_kernel(cap, own, rows_ref, sent_ref, give_ref):
    _, slots, toks = give_ref.shape
    width = sent_ref.shape[3]
    mine = lax.axis_index("zh")
    z = mine * QUAD + lax.axis_index("zl")
    r = iota((slots, LANES), 0)
    wanted = flag((r // (cap * QUAD)) * ZS + z == iota((slots, LANES), 1))
    i, j = iota((toks, toks), 0), iota((toks, toks), 1)
    before = flag((i < j) & (i // own == j // own))
    rr, tt = iota((slots, toks), 0), iota((slots, toks), 1)
    for k in range(2):
        rows = rows_ref[:, k * own : (k + 1) * own, :].reshape(toks, -1)
        share_at = dot(wanted, rows[:, width:], ((1,), (1,)))
        earlier = dot(flag(share_at > 0), before)
        hit = (share_at > 0) & (tt // own == (rr // cap) % QUAD) & (earlier == (rr % cap).astype(F32))
        give_ref[k] = jnp.where(hit, share_at, 0.0).astype(BF)
        packed = dot(flag(hit), rows[:, :width]).astype(BF)
        sent_ref[:, pl.ds((mine + k) % 2, 1)] = packed.reshape(YS, 1, slots // YS, width)


def combine_kernel(give_ref, rows_ref, out_ref):
    mine = lax.axis_index("zh")
    slots = give_ref.shape[1]
    own = out_ref.shape[1] // 2
    for k in range(2):
        rows = rows_ref[:, pl.ds((mine + k) % 2, 1)].reshape(slots, -1)
        part = dot(give_ref[k], rows, ((0,), (0,))).astype(BF)
        out_ref[:, k * own : (k + 1) * own] = part.reshape(QUAD, own, -1)


def expert_kernel(rows_ref, kept_ref, gate_ref, up_hbm, down_hbm, out_ref, up, down, hidden, sems):
    ff, width = down.shape
    begun = []
    for src, dst, parts in ((down_hbm, down, DOWN_PARTS), (up_hbm, up, UP_PARTS)):
        step = src.shape[0] // parts
        for k in range(parts):
            at = pl.ds(k * step, step)
            copy = pltpu.make_async_copy(src.at[at], dst.at[at], sems.at[len(begun)])
            copy.start()
            begun.append((copy, at))
    for copy, at in begun[:DOWN_PARTS]:
        copy.wait()
        hidden[:, at] = dot(rows_ref[...], down[at, :], ((1,), (1,)))
    h = hidden[...]
    g = kept_ref[:, :ff].astype(F32)
    u = kept_ref[:, ff:].astype(F32)
    s = jax.nn.sigmoid(g)
    hs = h * s
    up_grad = (hs * g).astype(BF)
    gate_grad = (hs * u * (1.0 + g * (1.0 - s))).astype(BF)
    for copy, at in begun[DOWN_PARTS:]:
        copy.wait()
        total = dot(gate_grad, gate_ref[at, :], ((1,), (1,))) + dot(up_grad, up[at, :], ((1,), (1,)))
        out_ref[:, at] = total.astype(BF)


def sum_of(parts_ref, at):
    acc = parts_ref[0, at].astype(F32)
    for k in range(1, parts_ref.shape[0]):
        acc = acc + parts_ref[k, at].astype(F32)
    return acc


def half_kernel(parts_ref, out_ref):
    own = out_ref.shape[0]
    out_ref[...] = sum_of(parts_ref, slice(own, 2 * own)).astype(BF)


def total_kernel(parts_ref, far_ref, out_ref):
    own = out_ref.shape[0]
    out_ref[...] = (sum_of(parts_ref, slice(0, own)) + far_ref[...].astype(F32)).astype(BF)


def swapped(x):
    return lax.ppermute(x, "zh", [(0, 1), (1, 0)])


def quad(x):
    return lax.all_to_all(x, "zl", 0, 0, tiled=True)


def across(x):
    return lax.all_to_all(x.reshape(YS, -1, x.shape[-1]), "y", 0, 0, tiled=True).reshape(x.shape)


def body(cotangent, expert_ids, gate_probs, saved, w_gate, w_up, w_down):
    sections = lax.axis_size("section")
    tokens, width = cotangent.shape[1:]
    slots = saved.shape[2]
    cap = slots // (YS * ZS)
    half = QUAD * tokens
    incoming = lax.ppermute(cotangent[0], "section", [(i, (i - 1) % sections) for i in range(sections)])
    shares = call(shares_kernel, bf16(tokens, LANES), 4, (10**5, 10**4))(expert_ids[0], gate_probs[0])
    one = call(payload_kernel, bf16(tokens, width + LANES), 4, (10**5, 10**6))(incoming, shares)
    payload = call(copies_kernel, bf16(QUAD, 2 * tokens, width + LANES), 4, (10**5, 10**6))(one, swapped(one))
    sent, give = call(
        lambda *refs: pack_kernel(cap, tokens, *refs),
        (bf16(YS, 2, slots // (2 * YS), width), bf16(2, slots // 2, half)),
        8,
        (10**8, 10**6),
    )(quad(payload))
    vm = pl.BlockSpec(memory_space=pltpu.VMEM)
    anywhere = pl.BlockSpec(memory_space=pl.ANY)
    grads = pl.pallas_call(
        expert_kernel,
        out_shape=bf16(slots, width),
        in_specs=[vm, vm, vm, anywhere, anywhere],
        out_specs=vm,
        scratch_shapes=[
            pltpu.VMEM(w_up.shape[1:], BF),
            pltpu.VMEM(w_down.shape[1:], BF),
            pltpu.VMEM((slots, w_down.shape[1]), F32),
            pltpu.SemaphoreType.DMA((DOWN_PARTS + UP_PARTS,)),
        ],
        compiler_params=pltpu.CompilerParams(vmem_limit_bytes=48 * MIB),
        cost_estimate=pl.CostEstimate(flops=24 * 10**8, bytes_accessed=12 * 10**6, transcendentals=0),
    )(across(sent).reshape(slots, width), saved[0, 0], w_gate[0], w_up[0], w_down[0])
    back = across(grads).reshape(sent.shape)
    parts = quad(call(combine_kernel, bf16(QUAD, 2 * tokens, width), 8, (10**8, 10**6))(give, back))
    far = swapped(call(half_kernel, bf16(tokens, width), 4, (10**6, 10**6))(parts))
    out = call(total_kernel, bf16(tokens, width), 4, (10**6, 10**6))(parts, far)
    return out[None]


def solution(mesh):
    split = Mesh(mesh.devices.reshape(-1, YS, ZS // QUAD, QUAD), ("section", "y", "zh", "zl"))
    line = ("y", "zh", "zl")
    over = P("section", line, None)
    weight = P(line, None, None)
    in_specs = (over, over, over, P("section", line, None, None), weight, weight, weight)
    return jax.shard_map(body, mesh=split, in_specs=in_specs, out_specs=over, check_vma=False)
```

```python
import jax
import jax.numpy as jnp
from jax import lax
from jax.experimental import pallas as pl
from jax.experimental.pallas import tpu as pltpu
from jax.sharding import Mesh, PartitionSpec as P

BF = jnp.bfloat16
F32 = jnp.float32
YS = 4
ZS = 8
QUAD = 4
LANES = 128
MIB = 1 << 20
DOWN_PARTS = 2
UP_PARTS = 1


def call(kernel, outs, limit, cost):
    return pl.pallas_call(
        kernel,
        out_shape=outs,
        compiler_params=pltpu.CompilerParams(vmem_limit_bytes=limit * MIB),
        cost_estimate=pl.CostEstimate(flops=cost[0], bytes_accessed=cost[1], transcendentals=0),
    )


def bf16(*shape):
    return jax.ShapeDtypeStruct(shape, BF)


def iota(shape, dim):
    return lax.broadcasted_iota(jnp.int32, shape, dim)


def dot(a, b, dims=((1,), (0,))):
    return lax.dot_general(a, b, (dims, ((), ())), preferred_element_type=F32)


def flag(mask):
    return jnp.where(mask, 1.0, 0.0).astype(BF)


def shares_kernel(ids_ref, probs_ref, out_ref):
    shape = out_ref.shape
    expert = iota(shape, 1)
    acc = jnp.zeros(shape, F32)
    for k in range(ids_ref.shape[1]):
        acc = acc + jnp.where(ids_ref[:, k : k + 1] == expert, probs_ref[:, k : k + 1].astype(F32), 0.0)
    out_ref[...] = acc.astype(BF)


def payload_kernel(near_ref, far_ref, near_share_ref, far_share_ref, out_ref):
    own, width = near_ref.shape
    for k in range(QUAD):
        out_ref[k, :own, :width] = near_ref[...]
        out_ref[k, own:, :width] = far_ref[...]
        out_ref[k, :own, width:] = near_share_ref[...]
        out_ref[k, own:, width:] = far_share_ref[...]


def pack_kernel(cap, own, rows_ref, sent_ref, give_ref):
    _, slots, toks = give_ref.shape
    width = sent_ref.shape[3]
    mine = lax.axis_index("zh")
    z = mine * QUAD + lax.axis_index("zl")
    r = iota((slots, LANES), 0)
    wanted = flag((r // (cap * QUAD)) * ZS + z == iota((slots, LANES), 1))
    i, j = iota((toks, toks), 0), iota((toks, toks), 1)
    before = flag((i < j) & (i // own == j // own))
    rr, tt = iota((slots, toks), 0), iota((slots, toks), 1)
    for k in range(2):
        rows = rows_ref[:, k * own : (k + 1) * own, :].reshape(toks, -1)
        share_at = dot(wanted, rows[:, width:], ((1,), (1,)))
        earlier = dot(flag(share_at > 0), before)
        hit = (share_at > 0) & (tt // own == (rr // cap) % QUAD) & (earlier == (rr % cap).astype(F32))
        give_ref[k] = jnp.where(hit, share_at, 0.0).astype(BF)
        packed = dot(flag(hit), rows[:, :width]).astype(BF)
        sent_ref[:, pl.ds((mine + k) % 2, 1)] = packed.reshape(YS, 1, slots // YS, width)


def combine_kernel(give_ref, rows_ref, near_ref, far_ref):
    mine = lax.axis_index("zh")
    slots = give_ref.shape[1]
    for k, out_ref in ((1, far_ref), (0, near_ref)):
        rows = rows_ref[:, pl.ds((mine + k) % 2, 1)].reshape(slots, -1)
        out_ref[...] = dot(give_ref[k], rows, ((0,), (0,))).astype(BF)


def expert_kernel(rows_ref, kept_ref, gate_ref, up_hbm, down_hbm, out_ref, up, down, hidden, sems):
    ff, width = down.shape
    begun = []
    for src, dst, parts in ((down_hbm, down, DOWN_PARTS), (up_hbm, up, UP_PARTS)):
        step = src.shape[0] // parts
        for k in range(parts):
            at = pl.ds(k * step, step)
            copy = pltpu.make_async_copy(src.at[at], dst.at[at], sems.at[len(begun)])
            copy.start()
            begun.append((copy, at))
    for copy, at in begun[:DOWN_PARTS]:
        copy.wait()
        hidden[:, at] = dot(rows_ref[...], down[at, :], ((1,), (1,)))
    h = hidden[...]
    g = kept_ref[:, :ff].astype(F32)
    u = kept_ref[:, ff:].astype(F32)
    s = jax.nn.sigmoid(g)
    hs = h * s
    up_grad = (hs * g).astype(BF)
    gate_grad = (hs * u * (1.0 + g * (1.0 - s))).astype(BF)
    for copy, at in begun[DOWN_PARTS:]:
        copy.wait()
        total = dot(gate_grad, gate_ref[at, :], ((1,), (1,))) + dot(up_grad, up[at, :], ((1,), (1,)))
        out_ref[:, at] = total.astype(BF)


def sum_of(parts_ref):
    acc = parts_ref[0].astype(F32)
    for k in range(1, parts_ref.shape[0]):
        acc = acc + parts_ref[k].astype(F32)
    return acc


def half_kernel(parts_ref, out_ref):
    out_ref[...] = sum_of(parts_ref).astype(BF)


def total_kernel(parts_ref, far_ref, out_ref):
    out_ref[...] = (sum_of(parts_ref) + far_ref[...].astype(F32)).astype(BF)


def swapped(x):
    return lax.ppermute(x, "zh", [(0, 1), (1, 0)])


def quad(x):
    return lax.all_to_all(x, "zl", 0, 0, tiled=True)


def across(x):
    return lax.all_to_all(x.reshape(YS, -1, x.shape[-1]), "y", 0, 0, tiled=True).reshape(x.shape)


def body(cotangent, expert_ids, gate_probs, saved, w_gate, w_up, w_down):
    sections = lax.axis_size("section")
    tokens, width = cotangent.shape[1:]
    slots = saved.shape[2]
    cap = slots // (YS * ZS)
    half = QUAD * tokens
    halves = ZS // QUAD
    moves = [
        ((q * halves + h) * QUAD + k, ((q - 1) % sections * halves + (h + 1) % halves) * QUAD + k)
        for q in range(sections)
        for h in range(halves)
        for k in range(QUAD)
    ]
    crossed = lax.ppermute(cotangent[0], ("section", "zh", "zl"), moves)
    incoming = lax.ppermute(cotangent[0], "section", [(i, (i - 1) % sections) for i in range(sections)])
    shares = call(shares_kernel, bf16(tokens, LANES), 4, (10**5, 10**4))(expert_ids[0], gate_probs[0])
    payload = call(payload_kernel, bf16(QUAD, 2 * tokens, width + LANES), 4, (10**5, 10**6))(
        incoming, crossed, shares, swapped(shares)
    )
    sent, give = call(
        lambda *refs: pack_kernel(cap, tokens, *refs),
        (bf16(YS, 2, slots // (2 * YS), width), bf16(2, slots // 2, half)),
        8,
        (10**8, 10**6),
    )(quad(payload))
    vm = pl.BlockSpec(memory_space=pltpu.VMEM)
    anywhere = pl.BlockSpec(memory_space=pl.ANY)
    grads = pl.pallas_call(
        expert_kernel,
        out_shape=bf16(slots, width),
        in_specs=[vm, vm, vm, anywhere, anywhere],
        out_specs=vm,
        scratch_shapes=[
            pltpu.VMEM(w_up.shape[1:], BF),
            pltpu.VMEM(w_down.shape[1:], BF),
            pltpu.VMEM((slots, w_down.shape[1]), F32),
            pltpu.SemaphoreType.DMA((DOWN_PARTS + UP_PARTS,)),
        ],
        compiler_params=pltpu.CompilerParams(vmem_limit_bytes=48 * MIB),
        cost_estimate=pl.CostEstimate(flops=24 * 10**8, bytes_accessed=12 * 10**6, transcendentals=0),
    )(across(sent).reshape(slots, width), saved[0, 0], w_gate[0], w_up[0], w_down[0])
    back = across(grads).reshape(sent.shape)
    near, far = call(combine_kernel, (bf16(half, width), bf16(half, width)), 8, (10**8, 10**6))(give, back)
    far = quad(far.reshape(QUAD, tokens, width))
    far = swapped(call(half_kernel, bf16(tokens, width), 4, (10**6, 10**6))(far))
    near = quad(near.reshape(QUAD, tokens, width))
    out = call(total_kernel, bf16(tokens, width), 4, (10**6, 10**6))(near, far)
    return out[None]


def solution(mesh):
    split = Mesh(mesh.devices.reshape(-1, YS, ZS // QUAD, QUAD), ("section", "y", "zh", "zl"))
    line = ("y", "zh", "zl")
    over = P("section", line, None)
    weight = P(line, None, None)
    in_specs = (over, over, over, P("section", line, None, None), weight, weight, weight)
    return jax.shard_map(body, mesh=split, in_specs=in_specs, out_specs=over, check_vma=False)
```
